32 devices in a mesh: dp: 8 (over y, x, core), fsdp: 4 (over z).
Axes of the slice: x: 2, y: 2, z: 4, core: 2. Of those that a mesh axis runs over, the one named last changes fastest.
Arguments:
- grad_partial: bfloat16 [8, 1, 1024, 4096], P('dp', None, 'fsdp'), may hold values from -0.375 to 0.375
- factors: float32 [8, 1024, 1024], P('dp', 'fsdp'), may hold values from -1 to 11, as said below
- bases: float32 [8, 1024, 1024], P('dp', 'fsdp'), may hold values from -1 to 2, as said below
- first_moment: float32 [8, 1024, 512], P('dp', 'fsdp'), may hold values from -0.3125 to 0.3125
- second_moment: float32 [8, 1024, 512], P('dp', 'fsdp'), may hold values from 0.003 to 0.03
Outputs:
- new_factors: float32 [8, 1024, 1024], P('dp', 'fsdp')
- new_bases: bfloat16 [8, 1024, 1024], P('dp', 'fsdp')
- new_first: float32 [8, 1024, 512], P('dp', 'fsdp')
- new_second: float32 [8, 1024, 512], P('dp', 'fsdp')
- direction: bfloat16 [8, 1024, 512], P('dp', 'fsdp')
The draws below stay inside these ranges and needn't reach their ends.
Inputs may be any that keep to these rules, and one draw needn't show every extreme that they name: Each factors[t] is symmetric and positive definite. Each bases[t] is nonsingular.
All inputs are finite; a program needn't handle non-finite values.
Results may differ from the reference program's by a relative error of at most 0.024.
Values may be sent and summed in bfloat16 or wider, within the bound.
No kernel may reach another device: no remote copies, remote signals or barrier semaphores. Data moves between devices by JAX's collectives and lax.ppermute only.
A program may use at most 64 MiB of HBM per device.

```python
import math
import jax
import jax.numpy as jnp
from jax import lax

BLOCK = 1024
CB = 4
RB = 1
COLS = 4096
TASKS = 8
HALF = 512
N_DP = 8


def draw_factors(key, part):
    spread = 0.5
    low_diag = 2.5
    high_diag = 7.0
    amplitude = spread * math.sqrt(3.0) / math.sqrt(BLOCK)
    uniform_noise = jax.random.uniform(jax.random.fold_in(key, 11), (TASKS, BLOCK, BLOCK), jnp.float32, -amplitude, amplitude)
    symmetric = (uniform_noise + jnp.swapaxes(uniform_noise, 1, 2)) / math.sqrt(2.0)
    diagonal = jnp.exp(jax.random.uniform(jax.random.fold_in(key, 12), (TASKS, BLOCK), jnp.float32, math.log(low_diag), math.log(high_diag)))
    return symmetric + diagonal[:, :, None] * jnp.eye(BLOCK, dtype=jnp.float32)[None]


def draw_bases(key, part):
    spread = 0.15
    amplitude = spread * math.sqrt(3.0) / math.sqrt(BLOCK)
    noise_term = jax.random.uniform(jax.random.fold_in(key, 21), (TASKS, BLOCK, BLOCK), jnp.float32, -amplitude, amplitude)
    return noise_term + jnp.eye(BLOCK, dtype=jnp.float32)[None]


def raised(values, rng, source, target, parts, factor):
    owner, partner = [(jnp.arange(values.shape[position]) // (values.shape[position] // parts)).reshape([-1 if axis == position else 1 for axis in range(values.ndim)]) for position in (source, target)]
    chosen = jax.random.permutation(rng, parts)[partner]
    strong = (owner == chosen) | (owner == (partner + parts // 2) % parts)
    return jnp.where(strong, factor * values, values)


def block_levels(own_key, dims, pieces, smallest, largest):
    def one(position, parts):
        steps = jax.random.uniform(jax.random.fold_in(jax.random.fold_in(own_key, 6), position), (parts,), jnp.float32, smallest / len(pieces), largest / len(pieces))
        return jnp.repeat(jnp.exp(steps), dims[position] // parts).reshape((-1,) + (1,) * (len(dims) - position - 1))

    loudness = one(*pieces[0])
    for cut in pieces[1:]:
        loudness = loudness * one(*cut)
    return loudness


def centred(rng, shape, scale, limit, split=(), kind=jnp.bfloat16):
    result = jax.random.normal(rng, shape, jnp.float32) * scale
    if len(split) > 0:
        result = block_levels(rng, shape, split, -0.22, 0.18) * result
    return jnp.clip(result, min=-limit, max=limit).astype(kind)


def noise_with(own_key, extent, width, bound, pieces, heavy, kind=jnp.bfloat16):
    values = width * jax.random.normal(own_key, extent, jnp.float32)
    if pieces:
        values = values * block_levels(own_key, extent, pieces, -0.22, 0.18)
    return jnp.clip(raised(values, jax.random.fold_in(own_key, 3), *heavy), -bound, bound).astype(kind)


def setup_inputs(seed: int = 0) -> dict:
    keys = jax.random.split(jax.random.key(seed), 6)
    return {
        "grad_partial": noise_with(keys[0], (N_DP, RB, BLOCK, COLS), (4.0 / (BLOCK * N_DP) ** 0.5), 0.375, ((0, 8), (2, 4)), (0, 3, 8, 2.0)),
        "factors": draw_factors(jax.random.fold_in(keys[5], 71), 0),
        "bases": draw_bases(jax.random.fold_in(keys[5], 71), 0),
        "first_moment": centred(keys[3], (TASKS, BLOCK, HALF), 0.05, 0.3125, ((0, 8), (1, 4)), jnp.float32),
        "second_moment": jnp.clip(jnp.exp(math.log(0.03) - 2.3025851 * jax.random.uniform(keys[4], (TASKS, BLOCK, HALF), jnp.float32) ** block_levels(keys[4], (TASKS, BLOCK, HALF), ((0, 8), (1, 4)), -0.2, 0.2)), 0.003, 0.03),
    }


def refresh(factor_now, basis_old):
    power_rows = jnp.dot(factor_now.astype(jnp.float32), basis_old.astype(jnp.float32), precision=lax.Precision.HIGHEST, preferred_element_type=jnp.float32)
    gram_matrix = jnp.dot(power_rows.T.astype(jnp.float32), power_rows.astype(jnp.float32), precision=lax.Precision.HIGHEST, preferred_element_type=jnp.float32)
    lower_factor = jnp.linalg.cholesky(gram_matrix)
    solved = lax.linalg.triangular_solve(lower_factor, power_rows, left_side=False, lower=True, transpose_a=True)
    return solved.astype(jnp.bfloat16)

def one_block(arguments):
    block_tile, factor_pair, basis_pair, first_old, second_old = arguments
    left_factor = 0.95 * factor_pair[0] + 0.05 * jnp.dot(block_tile.astype(jnp.float32), block_tile.T.astype(jnp.float32), preferred_element_type=jnp.float32)
    right_factor = 0.95 * factor_pair[1] + 0.05 * jnp.dot(block_tile.T.astype(jnp.float32), block_tile.astype(jnp.float32), preferred_element_type=jnp.float32)
    left_basis = refresh(left_factor, basis_pair[0])
    right_basis = refresh(right_factor, basis_pair[1])
    mixed_rows = jnp.dot(left_basis.T.astype(jnp.float32), block_tile.astype(jnp.float32), preferred_element_type=jnp.float32).astype(jnp.bfloat16)
    rotated = jnp.dot(mixed_rows.astype(jnp.float32), right_basis.astype(jnp.float32), preferred_element_type=jnp.float32)
    rotated = jnp.stack([rotated[:, :HALF], rotated[:, HALF:]])
    first_new = 0.95 * first_old + 0.05 * rotated
    second_new = 0.95 * second_old + 0.05 * rotated * rotated
    normalized = (first_new / (jnp.sqrt(second_new) + 1e-08)).astype(jnp.bfloat16)
    joined = jnp.concatenate([normalized[0], normalized[1]], axis=1)
    weighted = jnp.dot(left_basis.astype(jnp.float32), joined.astype(jnp.float32), preferred_element_type=jnp.float32).astype(jnp.bfloat16)
    combined = jnp.dot(weighted.astype(jnp.float32), right_basis.T.astype(jnp.float32), preferred_element_type=jnp.float32).astype(jnp.bfloat16)
    combined = jnp.stack([combined[:, :HALF], combined[:, HALF:]])
    return (jnp.stack([left_factor, right_factor]), jnp.stack([left_basis, right_basis]), first_new, second_new, combined)

def paired(array_value):
    return array_value.reshape((RB * CB, 2) + array_value.shape[1:])

def unpaired(array_value):
    return array_value.reshape((TASKS,) + array_value.shape[2:])

def reference(grad_partial, factors, bases, first_moment, second_moment):
    summed = lax.optimization_barrier(jnp.sum(grad_partial, axis=0, dtype=jnp.float32)).astype(jnp.bfloat16)
    blocks = summed.reshape(RB, BLOCK, CB, BLOCK).transpose(0, 2, 1, 3).reshape(RB * CB, BLOCK, BLOCK)
    results = lax.map(one_block, (blocks, paired(factors), paired(bases), paired(first_moment), paired(second_moment)))
    return (unpaired(results[0]), unpaired(results[1]), unpaired(results[2]), unpaired(results[3]), unpaired(results[4]))
```

```python
import functools

import jax
import jax.numpy as jnp
from jax import lax
from jax.experimental import pallas as pl
from jax.experimental.pallas import tpu as pltpu
from jax.sharding import PartitionSpec as P

TILE = 128
SUB = 8
VMEM_GRANT = 60 * 2**20


def splat_lane(x, lane):
    return jnp.broadcast_to(x[:, lane : lane + 1], x.shape)


def splat_row(x, row):
    return jnp.broadcast_to(x[row : row + 1, :], x.shape)


def reciprocal(x):
    guess = pl.reciprocal(x, approx=True)
    return guess * (2.0 - x * guess)


def tree_sum(terms):
    while len(terms) > 1:
        terms = [x + y for x, y in zip(terms[0::2], terms[1::2])]
    return terms[0]


def inverse_columns(columns, sub):
    held = list(columns)
    for p in range(0, SUB, 2):
        first, second = held[p], held[p + 1]
        a, b, c = splat_row(first, p), splat_row(second, p), splat_row(second, p + 1)
        det = reciprocal(a * c - b * b)
        ia, ib, ic = c * det, -b * det, a * det
        at_first, at_second = sub == p, sub == p + 1
        for k in range(SUB):
            if k == p:
                s, t = ia, ib
                kept = jnp.zeros_like(first)
            elif k == p + 1:
                s, t = ib, ic
                kept = jnp.zeros_like(first)
            else:
                u, v = splat_row(held[k], p), splat_row(held[k], p + 1)
                s, t = ia * u + ib * v, ib * u + ic * v
                kept = held[k]
            rest = kept - (first * s + second * t)
            held[k] = jnp.where(at_first, s, jnp.where(at_second, t, rest))
    return held


def scaled_rows(columns, rows, sub):
    columns = list(columns)
    for p in range(SUB):
        pivot = splat_row(columns[p], p)
        scale = lax.rsqrt(pivot)
        factor = jnp.where(sub > p, columns[p] * (scale * scale), 0.0)
        for k in range(p + 1, SUB):
            columns[k] = columns[k] - factor * splat_row(columns[k], p)
        rows = jnp.where(sub == p, rows * scale, rows - factor * splat_row(rows, p))
    return rows


def tile_inverse(tile):
    size = tile.shape[0]
    count = size // SUB
    lane = lax.broadcasted_iota(jnp.int32, (SUB, size), 1)
    sub = lax.broadcasted_iota(jnp.int32, (SUB, size), 0)
    groups = [tile[SUB * g : SUB * (g + 1), :] for g in range(count)]
    result = []
    for g in range(count):
        base = SUB * g
        in_block = (lane >= base) & (lane < base + SUB)
        pivots = [splat_lane(groups[g], base + k) for k in range(SUB)]
        inverse = inverse_columns(pivots, sub)
        one = jnp.where(lane == base + sub, 1.0, 0.0)
        own = jnp.where(in_block, one, groups[g])
        result.append(scaled_rows(pivots, jnp.where(lane < base, groups[g], one), sub))
        if g == count - 1:
            break
        applied = tree_sum([inverse[k] * splat_row(own, k) for k in range(SUB)])
        spread = [splat_row(applied, k) for k in range(SUB)]
        for h in range(g + 1, count):
            taken = tree_sum([splat_lane(groups[h], base + k) * spread[k] for k in range(SUB)])
            groups[h] = jnp.where(in_block, 0.0, groups[h]) - taken
    return jnp.concatenate(result, axis=0)


def split_cat(x, which, axis):
    hi = x.astype(jnp.bfloat16)
    lo = (x - hi.astype(jnp.float32)).astype(jnp.bfloat16)
    return jnp.concatenate([hi if w == "h" else lo for w in which], axis=axis)


def product(x, y, dims):
    return lax.dot_general(x, y, (dims, ((), ())), preferred_element_type=jnp.float32)


def product3(x, y, dims):
    (cx,), (cy,) = dims
    return product(split_cat(x, "hhl", cx), split_cat(y, "hlh", cy), dims)


NN, NT, TN = ((1,), (0,)), ((1,), (1,)), ((0,), (0,))


def invert_factor(ref):
    order = ref.shape[0]
    tiles = order // TILE
    lane = lax.broadcasted_iota(jnp.int32, (TILE, order), 1)
    row = lax.broadcasted_iota(jnp.int32, (TILE, order), 0)

    def step(j, carry):
        start = pl.multiple_of(j * TILE, TILE)
        rows = pl.ds(start, TILE)
        inverse = tile_inverse(ref[rows, rows])
        in_tile = (lane >= start) & (lane < start + TILE)
        whole = jnp.where(in_tile, jnp.where(lane - start == row, 1.0, 0.0), ref[rows, :])
        reduced = product3(inverse, whole, NN)
        ref[rows, :] = jnp.where(lane < start + TILE, reduced, 0.0)
        right = split_cat(reduced, "hlh", 0)

        def update(i, c):
            below = pl.ds(pl.multiple_of(i * TILE, TILE), TILE)
            left = product3(ref[below, rows], inverse, NT)
            kept = jnp.where(in_tile, 0.0, ref[below, :])
            ref[below, :] = kept - product(split_cat(left, "hhl", 1), right, NN)
            return c

        lax.fori_loop(j + 1, tiles, update, 0)
        return carry

    lax.fori_loop(0, tiles, step, 0)


HBM = pl.BlockSpec(memory_space=pl.ANY)
SMEM = pl.BlockSpec(memory_space=pltpu.SMEM)


def kernel_call(kernel, name, out_shape, scratch, flops, operands):
    return pl.pallas_call(
        kernel,
        out_shape=out_shape,
        in_specs=[SMEM] + [HBM] * (len(operands) - 1),
        out_specs=jax.tree.map(lambda _: HBM, out_shape),
        scratch_shapes=scratch,
        cost_estimate=pl.CostEstimate(flops=flops, bytes_accessed=16 * 2**20, transcendentals=0),
        compiler_params=pltpu.CompilerParams(vmem_limit_bytes=VMEM_GRANT),
        name=name,
    )(*operands)


class Copies:
    def __init__(self, semaphores):
        self.semaphores, self.used = semaphores, 0

    def start(self, source, target):
        copy = pltpu.make_async_copy(source, target, self.semaphores.at[self.used])
        self.used += 1
        copy.start()
        return copy

    def start_either(self, first, zero_source, one_source, target):
        semaphore = self.semaphores.at[self.used]
        self.used += 1

        @pl.when(first)
        def _():
            pltpu.make_async_copy(zero_source, target, semaphore).start()

        @pl.when(jnp.logical_not(first))
        def _():
            pltpu.make_async_copy(one_source, target, semaphore).start()

        return pltpu.make_async_copy(zero_source, target, semaphore)


def rows_from(position, distance, row_count, count):
    source = lax.rem(position - distance + count, count)
    return pl.ds(pl.multiple_of(source * row_count, row_count), row_count)


def orthonormalize(power_ref, q_ref, gram_ref):
    bf16 = jnp.bfloat16
    width = gram_ref.shape[0]
    for start in range(0, power_ref.shape[1], width):
        span = slice(start, start + width)
        group = power_ref[:, span]
        if start > 0:
            along = product(q_ref[:, :start], group.astype(bf16), TN).astype(bf16)
            group = group - product(q_ref[:, :start], along, NN)
        group = group.astype(bf16)
        gram_ref[...] = product(group, group, TN)
        invert_factor(gram_ref)
        inverse = split_cat(gram_ref[...], "hl", 1)
        q_ref[:, span] = product(jnp.concatenate([group, group], axis=1), inverse, NT).astype(bf16)


def share_kernel(symmetric, place_ref, factor_ref, basis_ref, share_ref):
    row_count, order = factor_ref.shape
    count = order // row_count
    width = order // 4
    bf16 = jnp.bfloat16
    shared = share_ref.shape[1] - width
    share_ref[:, shared:] = basis_ref[:, width : 2 * width].astype(bf16)
    if not symmetric:
        share_ref[:, :shared] = factor_ref[...].astype(bf16)
        return
    half = row_count // 2
    for r in range(count):

        @pl.when(place_ref[1] == r)
        def _():
            for offset in range(count // 2):
                start = (r + offset) % count * row_count
                share_ref[:, offset * row_count : (offset + 1) * row_count] = factor_ref[
                    :, start : start + row_count
                ].astype(bf16)
            start = (r + count // 2) % count * row_count
            if r < count // 2:
                last = factor_ref[:, start : start + half]
            else:
                last = factor_ref[half:, start : start + row_count].T
            share_ref[:, count // 2 * row_count : shared] = last.astype(bf16)


def gather_share(place, factor_rows, basis_rows, symmetric):
    row_count, order = factor_rows.shape
    shared = order // 2 + row_count // 2 if symmetric else order
    vmem = pl.BlockSpec(memory_space=pltpu.VMEM)
    return pl.pallas_call(
        functools.partial(share_kernel, symmetric),
        out_shape=jax.ShapeDtypeStruct((row_count, shared + order // 4), jnp.bfloat16),
        in_specs=[SMEM, vmem, vmem],
        out_specs=vmem,
        cost_estimate=pl.CostEstimate(flops=0, bytes_accessed=3 * 2**20, transcendentals=0),
        compiler_params=pltpu.CompilerParams(vmem_limit_bytes=VMEM_GRANT),
        name="gather_share",
    )(place, factor_rows, basis_rows)


def first_kernel(half_steps, count, place_ref, gathered_hbm, rows_hbm, *refs):
    own, other, basis = refs[:count], refs[count : 2 * count], refs[2 * count : 3 * count]
    whole_hbm, new_rows_hbm, q_hbm = refs[3 * count : 3 * count + 3]
    block, old, columns, rows, whole, new_rows, power, q, gram, semaphores = refs[3 * count + 3 :]
    row_count, order = rows.shape
    half_width = order // 2
    width = order // 4
    shared = old.shape[1]
    first = place_ref[0] == 0
    copies = Copies(semaphores)
    waits, late = [], []
    for k in range(count):
        span = rows_from(place_ref[1], k, row_count, count)
        waits.append(copies.start_either(first, own[k], other[k], block.at[span, pl.ds(0, half_width)]))
        waits.append(copies.start_either(first, other[k], own[k], block.at[span, pl.ds(half_width, half_width)]))
    waits.append(copies.start(gathered_hbm.at[:, pl.ds(0, shared)], old))
    waits.append(copies.start(rows_hbm, rows))
    late.append(copies.start(gathered_hbm.at[:, pl.ds(shared, width)], columns.at[:, pl.ds(width, width)]))
    for k in range(count):
        span = rows_from(place_ref[1], k, row_count, count)
        late.append(copies.start(basis[k], columns.at[span, pl.ds(0, width)]))
    for copy in waits:
        copy.wait()

    def old_block(r, c):
        offset = (c - r) % count
        row = slice(r * row_count, (r + 1) * row_count)
        if half_steps is None:
            return old[row, c * row_count : (c + 1) * row_count].astype(jnp.float32)
        if offset < half_steps:
            return old[row, offset * row_count : (offset + 1) * row_count].astype(jnp.float32)
        if offset > half_steps or r >= half_steps:
            return old_block(c, r).T
        mirror = slice(c * row_count, (c + 1) * row_count)
        part = slice(half_steps * row_count, half_steps * row_count + row_count // 2)
        return jnp.concatenate([old[row, part], old[mirror, part]], axis=1).astype(jnp.float32)

    @pl.when(first)
    def _():
        for start in range(0, order, width):
            power[start : start + width, :] = product(block[start : start + width, :], block[...], NT)

    @pl.when(jnp.logical_not(first))
    def _():
        for start in range(0, order, width):
            power[start : start + width, :] = product(block[:, start : start + width], block[...], TN)

    here = rows_from(place_ref[1], 0, row_count, count)
    new_rows[...] = 0.95 * rows[...] + 0.05 * power[here, :]
    for r in range(count):
        row = slice(r * row_count, (r + 1) * row_count)
        rest = jnp.concatenate([old_block(r, c) for c in range(count)], axis=1)
        whole[row, :] = (0.95 * rest + 0.05 * power[row, :]).astype(jnp.bfloat16)
    outputs = [copies.start(new_rows, new_rows_hbm), copies.start(whole, whole_hbm)]
    for copy in late:
        copy.wait()
    power[:, :half_width] = product(whole[...], columns[...], NN)
    orthonormalize(power.at[:, pl.ds(0, half_width)], q, gram)
    outputs.append(copies.start(q, q_hbm))
    for copy in outputs:
        copy.wait()


def first_half(place, own, other, basis, gathered, rows, half_steps):
    row_count, order = rows.shape
    count = len(own)
    half = order // 2
    bf16, f32 = jnp.bfloat16, jnp.float32
    shape, vmem = jax.ShapeDtypeStruct, pltpu.VMEM
    return kernel_call(
        functools.partial(first_kernel, half_steps, count),
        "first_half",
        (shape((order, order), bf16), shape(rows.shape, f32), shape((order, half), bf16)),
        [
            vmem((order, order), bf16),
            vmem((order, gathered.shape[1] - order // 4), bf16),
            vmem((order, half), bf16),
            vmem(rows.shape, f32),
            vmem((order, order), bf16),
            vmem(rows.shape, f32),
            vmem((order, order), f32),
            vmem((order, half), bf16),
            vmem((half // 2, half // 2), f32),
            pltpu.SemaphoreType.DMA((3 * count + 6,)),
        ],
        6 * order**3,
        (place, gathered, rows, *own, *other, *basis),
    )


def second_kernel(count, place_ref, whole_hbm, before_hbm, *refs):
    basis, (q_hbm, rows_hbm) = refs[:count], refs[count : count + 2]
    whole, before, columns, power, q, gram, semaphores = refs[count + 2 :]
    order, half = before.shape
    row_count = order // count
    bf16 = jnp.bfloat16
    here = rows_from(place_ref[1], 0, row_count, count)
    copies = Copies(semaphores)
    waits = [copies.start(whole_hbm, whole)]
    for k in range(count):
        waits.append(copies.start(basis[k], columns.at[rows_from(place_ref[1], k, row_count, count), :]))
    last = copies.start(before_hbm, before)
    for copy in waits:
        copy.wait()
    power[...] = product(whole[...], columns[...], NN)
    last.wait()
    outputs = [copies.start(before.at[here, :], rows_hbm.at[:, pl.ds(0, half)])]
    along = product(before[...], power[...].astype(bf16), TN)
    power[...] = power[...] - product(before[...], along.astype(bf16), NN)
    orthonormalize(power, q, gram)
    outputs.append(copies.start(q, q_hbm))
    outputs.append(copies.start(q.at[here, :], rows_hbm.at[:, pl.ds(half, half)]))
    for copy in outputs:
        copy.wait()


def second_half(place, basis, whole, before):
    order, half = before.shape
    row_count = order // len(basis)
    bf16, f32 = jnp.bfloat16, jnp.float32
    shape, vmem = jax.ShapeDtypeStruct, pltpu.VMEM
    return kernel_call(
        functools.partial(second_kernel, len(basis)),
        "second_half",
        (shape((order, half), bf16), shape((row_count, order), bf16)),
        [
            vmem((order, order), bf16),
            vmem((order, half), bf16),
            vmem((order, half), bf16),
            vmem((order, half), f32),
            vmem((order, half), bf16),
            vmem((half // 2, half // 2), f32),
            pltpu.SemaphoreType.DMA((len(basis) + 5,)),
        ],
        4 * order**3,
        (place, whole, before, *basis),
    )


def moment_kernel(count, place_ref, *refs):
    own, other, own_pieces, other_pieces = refs[:2], refs[2:4], refs[4 : 4 + count], refs[4 + count : 4 + 2 * count]
    moments_hbm, first_hbm, second_hbm = refs[4 + 2 * count : 7 + 2 * count]
    weighted_hbm, first_out, second_out = refs[7 + 2 * count : 10 + 2 * count]
    left, right, block, moments, first_rows, second_rows, mixed, rotated, normal, weighted, semaphores = refs[
        10 + 2 * count :
    ]
    row_count, half_width = first_rows.shape
    order = left.shape[0]
    f32, bf16 = jnp.float32, jnp.bfloat16
    first = place_ref[0] == 0
    here = rows_from(place_ref[1], 0, row_count, count)
    upper, lower = pl.ds(0, half_width), pl.ds(half_width, half_width)
    copies = Copies(semaphores)
    early = [copies.start_either(first, other[0], own[1], right)]
    for k in range(count):
        span = rows_from(place_ref[1], k, row_count, count)
        early.append(copies.start_either(first, own_pieces[k], other_pieces[k], block.at[span, upper]))
        early.append(copies.start_either(first, other_pieces[k], own_pieces[k], block.at[span, lower]))
    late = [
        copies.start_either(first, own[0], other[0], left.at[:, upper]),
        copies.start_either(first, own[1], other[1], left.at[:, lower]),
        copies.start(moments_hbm, moments),
        copies.start(first_hbm, first_rows),
        copies.start(second_hbm, second_rows),
    ]
    for copy in early:
        copy.wait()
    mixed[...] = product(block[...], right[...], NN).astype(bf16)
    for copy in late:
        copy.wait()
    total = jnp.zeros(weighted.shape, f32)
    width = order // 4
    for start in range(0, order, width):
        span = slice(start, start + width)
        turn = product(left[:, span], mixed[...], TN)
        rotated[span, :] = turn
        new_first = 0.95 * moments[span, :half_width].astype(f32) + 0.05 * turn
        new_second = 0.95 * moments[span, half_width:].astype(f32) + 0.05 * turn * turn
        normal[span, :] = (new_first / (jnp.sqrt(new_second) + 1e-08)).astype(bf16)
        total = total + product(left[here, span], normal[span, :], NN)
    weighted[...] = total.astype(bf16)
    outputs = [copies.start(weighted, weighted_hbm)]
    turn = rotated[here, :]
    first_rows[...] = 0.95 * first_rows[...] + 0.05 * turn
    second_rows[...] = 0.95 * second_rows[...] + 0.05 * turn * turn
    outputs += [copies.start(first_rows, first_out), copies.start(second_rows, second_out)]
    for copy in outputs:
        copy.wait()


def moment_step(place, own, other, own_pieces, other_pieces, moments, first, second):
    order = own[0].shape[0]
    half = first.shape[1]
    count = len(own_pieces)
    f32, bf16 = jnp.float32, jnp.bfloat16
    shape, vmem = jax.ShapeDtypeStruct, pltpu.VMEM
    return kernel_call(
        functools.partial(moment_kernel, count),
        "moment_step",
        (shape(first.shape, bf16), shape(first.shape, f32), shape(first.shape, f32)),
        [
            vmem((order, order), bf16),
            vmem((order, half), bf16),
            vmem((order, order), bf16),
            vmem((order, order), bf16),
            vmem(first.shape, f32),
            vmem(first.shape, f32),
            vmem((order, half), bf16),
            vmem((order, half), f32),
            vmem((order, half), bf16),
            vmem(first.shape, bf16),
            pltpu.SemaphoreType.DMA((2 * count + 9,)),
        ],
        4 * order * order * half,
        (place, *own, *other, *own_pieces, *other_pieces, moments, first, second),
    )


def direction_kernel(place_ref, *refs):
    own, other, (mine_hbm, theirs_hbm, out_hbm) = refs[:2], refs[2:4], refs[4:7]
    near, far, mine, theirs, out, semaphores = refs[7:]
    half = near.shape[0]
    upper, lower = pl.ds(0, half), pl.ds(half, half)
    first = place_ref[0] == 0
    copies = Copies(semaphores)
    waits = [
        copies.start(mine_hbm, mine),
        copies.start(theirs_hbm, theirs),
        copies.start_either(first, other[0].at[upper, :], own[1].at[lower, :], near),
        copies.start_either(first, other[1].at[upper, :], own[0].at[lower, :], far),
    ]
    for copy in waits:
        copy.wait()
    out[...] = (product(mine[...], near[...], NT) + product(theirs[...], far[...], NT)).astype(out.dtype)
    copies.start(out, out_hbm).wait()


def direction_step(place, own, other, mine, theirs):
    half = mine.shape[1]
    vmem = pltpu.VMEM
    square, rows = vmem((half, half), mine.dtype), vmem(mine.shape, mine.dtype)
    return kernel_call(
        direction_kernel,
        "direction_step",
        jax.ShapeDtypeStruct(mine.shape, mine.dtype),
        [square, square, rows, rows, rows, pltpu.SemaphoreType.DMA((5,))],
        4 * mine.shape[0] * half * half,
        (place, *own, *other, mine, theirs),
    )


def exchanged(block, axis, partner_of):
    count = lax.axis_size(axis)
    return lax.ppermute(block, axis, [(i, partner_of(i)) for i in range(count)])


def sibling(block):
    return exchanged(block, "dp", lambda i: i ^ 1)


def rounded_sum(x, y):
    return (x.astype(jnp.float32) + y.astype(jnp.float32)).astype(jnp.bfloat16)


def reversed_bits(value, bits):
    return sum(((value >> k) & 1) << (bits - 1 - k) for k in range(bits))


def pair_terms(partial_rows, half_width):
    side = lax.axis_index("dp") % 2
    blocks = lax.axis_size("dp") // 2
    bits = blocks.bit_length() - 1
    row_blocks, _, columns = partial_rows.shape
    halves = [
        partial_rows[rb, :, start : start + half_width]
        for rb in range(row_blocks)
        for start in range(0, columns, half_width)
    ]
    lows, highs = halves[0::2], halves[1::2]
    turned = [reversed_bits(k, bits) for k in range(blocks)]
    keep = jnp.stack([jnp.where(side == 0, lows[k], highs[turned[k]]) for k in range(blocks)])
    send = jnp.stack([jnp.where(side == 0, highs[turned[k]], lows[k]) for k in range(blocks)])
    return send, keep


def reduced_half_block(held, ahead):
    position = lax.axis_index("dp")
    side = position % 2
    bits = held.shape[0].bit_length() - 1
    for step in range(bits):
        low_bit, high_bit = 1 + step, bits - step
        mine = jnp.where(side == 0, position >> high_bit, position >> low_bit) & 1
        middle = held.shape[0] // 2
        keep = jnp.where(mine == 0, held[:middle], held[middle:])
        send = jnp.where(mine == 0, held[middle:], held[:middle])
        if step == bits - 1:
            send, ahead = lax.optimization_barrier((send, ahead))
        arrived = exchanged(send, "dp", lambda i: i ^ (1 << (low_bit if i % 2 else high_bit)))
        held = rounded_sum(keep, arrived)
    return held[0], ahead


def pieces_by_distance(shard, axis):
    count = lax.axis_size(axis)
    return [shard] + [
        lax.ppermute(shard, axis, [(i, (i + distance) % count) for i in range(count)]) for distance in range(1, count)
    ]


def body(grad_partial, factors, bases, first_moment, second_moment):
    row_count, block_width = factors.shape[1:]
    half_width = block_width // 2
    width = block_width // 4
    side = lax.axis_index("dp") % 2
    position, count = lax.axis_index("fsdp"), lax.axis_size("fsdp")
    place = jnp.stack([side, position]).astype(jnp.int32)
    bf16 = jnp.bfloat16

    send, keep = pair_terms(grad_partial[0], half_width)
    symmetric = row_count % 256 == 0 and count % 2 == 0
    share = gather_share(place, factors[0], bases[0], symmetric)
    pair_sum, share, first_rows = lax.optimization_barrier(
        (rounded_sum(keep, sibling(send)), share, bases[0, :, :width].astype(bf16))
    )
    gathered = lax.all_gather(share, "fsdp", axis=0, tiled=True)
    first_pieces = pieces_by_distance(first_rows, "fsdp")
    own_half, first_pieces = reduced_half_block(pair_sum, first_pieces)
    own_pieces = pieces_by_distance(own_half, "fsdp")
    other_pieces = [sibling(piece) for piece in own_pieces]

    moments = jnp.concatenate([first_moment[0].astype(bf16), second_moment[0].astype(bf16)], axis=1)
    rest, moments, own_pieces = lax.optimization_barrier((bases[0, :, half_width:].astype(bf16), moments, own_pieces))
    rest_pieces = pieces_by_distance(rest, "fsdp")
    moments = lax.all_gather(moments, "fsdp", axis=0, tiled=True)

    factor_whole, new_factor_rows, first_q = first_half(
        place, own_pieces, other_pieces, first_pieces, gathered, factors[0], count // 2 if symmetric else None
    )
    first_other = sibling(first_q)
    second_q, new_rows = second_half(place, rest_pieces, factor_whole, first_q)
    own, other = (first_q, second_q), (first_other, sibling(second_q))
    weighted, first_new, second_new = moment_step(
        place, own, other, own_pieces, other_pieces, moments, first_moment[0], second_moment[0]
    )
    direction = direction_step(place, own, other, weighted, sibling(weighted))
    return (new_factor_rows[None], new_rows[None], first_new[None], second_new[None], direction[None])


def solution(mesh):
    rows = P("dp", "fsdp", None)
    return jax.shard_map(
        body,
        mesh=mesh,
        in_specs=(P("dp", None, "fsdp", None), rows, rows, rows, rows),
        out_specs=(rows,) * 5,
        check_vma=False,
    )
```

```python
import functools

import jax
import jax.numpy as jnp
from jax import lax
from jax.experimental import pallas as pl
from jax.experimental.pallas import tpu as pltpu
from jax.sharding import PartitionSpec as P

TILE = 128
SUB = 8
VMEM_GRANT = 60 * 2**20


def splat_lane(x, lane):
    return jnp.broadcast_to(x[:, lane : lane + 1], x.shape)


def splat_row(x, row):
    return jnp.broadcast_to(x[row : row + 1, :], x.shape)


def reciprocal(x):
    guess = pl.reciprocal(x, approx=True)
    return guess * (2.0 - x * guess)


def tree_sum(terms):
    while len(terms) > 1:
        terms = [x + y for x, y in zip(terms[0::2], terms[1::2])]
    return terms[0]


def inverse_columns(columns, sub):
    held = list(columns)
    for p in range(0, SUB, 2):
        first, second = held[p], held[p + 1]
        a, b, c = splat_row(first, p), splat_row(second, p), splat_row(second, p + 1)
        inverse = reciprocal(a * c - b * b)
        at_first, at_second = sub == p, sub == p + 1
        left = jnp.where(at_first, -c, jnp.where(at_second, b, c * first - b * second))
        right = jnp.where(at_first, b, jnp.where(at_second, -a, a * second - b * first))
        for k in range(SUB):
            if k == p:
                held[k] = -left * inverse
            elif k == p + 1:
                held[k] = -right * inverse
            else:
                taken = left * splat_row(held[k], p) + right * splat_row(held[k], p + 1)
                held[k] = jnp.where(at_first | at_second, 0.0, held[k]) - taken * inverse
    return held


def scaled_rows(columns, rows, sub):
    columns = list(columns)
    for p in range(SUB):
        pivot = splat_row(columns[p], p)
        scale = lax.rsqrt(pivot)
        factor = jnp.where(sub > p, columns[p] * (scale * scale), 0.0)
        for k in range(p + 1, SUB):
            columns[k] = columns[k] - factor * splat_row(columns[k], p)
        rows = jnp.where(sub == p, rows * scale, rows - factor * splat_row(rows, p))
    return rows


def tile_inverse(tile):
    size = tile.shape[0]
    count = size // SUB
    lane = lax.broadcasted_iota(jnp.int32, (SUB, size), 1)
    sub = lax.broadcasted_iota(jnp.int32, (SUB, size), 0)
    groups = [tile[SUB * g : SUB * (g + 1), :] for g in range(count)]
    result = []
    for g in range(count):
        base = SUB * g
        in_block = (lane >= base) & (lane < base + SUB)
        pivots = [splat_lane(groups[g], base + k) for k in range(SUB)]
        inverse = inverse_columns(pivots, sub)
        one = jnp.where(lane == base + sub, 1.0, 0.0)
        own = jnp.where(in_block, one, groups[g])
        result.append(scaled_rows(pivots, jnp.where(lane < base, groups[g], one), sub))
        if g == count - 1:
            break
        applied = tree_sum([inverse[k] * splat_row(own, k) for k in range(SUB)])
        spread = [splat_row(applied, k) for k in range(SUB)]
        for h in range(g + 1, count):
            taken = tree_sum([splat_lane(groups[h], base + k) * spread[k] for k in range(SUB)])
            groups[h] = jnp.where(in_block, 0.0, groups[h]) - taken
    return jnp.concatenate(result, axis=0)


def split_cat(x, which, axis):
    hi = x.astype(jnp.bfloat16)
    lo = (x - hi.astype(jnp.float32)).astype(jnp.bfloat16)
    return jnp.concatenate([hi if w == "h" else lo for w in which], axis=axis)


def product(x, y, dims):
    return lax.dot_general(x, y, (dims, ((), ())), preferred_element_type=jnp.float32)


def product3(x, y, dims):
    (cx,), (cy,) = dims
    return product(split_cat(x, "hhl", cx), split_cat(y, "hlh", cy), dims)


NN, NT, TN = ((1,), (0,)), ((1,), (1,)), ((0,), (0,))


def invert_factor(ref):
    order = ref.shape[0]
    tiles = order // TILE
    lane = lax.broadcasted_iota(jnp.int32, (TILE, order), 1)
    row = lax.broadcasted_iota(jnp.int32, (TILE, order), 0)

    def step(j, carry):
        start = pl.multiple_of(j * TILE, TILE)
        rows = pl.ds(start, TILE)
        inverse = tile_inverse(ref[rows, rows])
        in_tile = (lane >= start) & (lane < start + TILE)
        whole = jnp.where(in_tile, jnp.where(lane - start == row, 1.0, 0.0), ref[rows, :])
        reduced = product3(inverse, whole, NN)
        ref[rows, :] = jnp.where(lane < start + TILE, reduced, 0.0)
        right = split_cat(reduced, "hlh", 0)

        def update(i, c):
            below = pl.ds(pl.multiple_of(i * TILE, TILE), TILE)
            left = product3(ref[below, rows], inverse, NT)
            kept = jnp.where(in_tile, 0.0, ref[below, :])
            ref[below, :] = kept - product(split_cat(left, "hhl", 1), right, NN)
            return c

        lax.fori_loop(j + 1, tiles, update, 0)
        return carry

    lax.fori_loop(0, tiles, step, 0)


HBM = pl.BlockSpec(memory_space=pl.ANY)
SMEM = pl.BlockSpec(memory_space=pltpu.SMEM)


def kernel_call(kernel, name, out_shape, scratch, flops, operands):
    return pl.pallas_call(
        kernel,
        out_shape=out_shape,
        in_specs=[SMEM] + [HBM] * (len(operands) - 1),
        out_specs=jax.tree.map(lambda _: HBM, out_shape),
        scratch_shapes=scratch,
        cost_estimate=pl.CostEstimate(flops=flops, bytes_accessed=16 * 2**20, transcendentals=0),
        compiler_params=pltpu.CompilerParams(vmem_limit_bytes=VMEM_GRANT),
        name=name,
    )(*operands)


class Copies:
    def __init__(self, semaphores):
        self.semaphores, self.used = semaphores, 0

    def start(self, source, target):
        copy = pltpu.make_async_copy(source, target, self.semaphores.at[self.used])
        self.used += 1
        copy.start()
        return copy

    def start_either(self, first, zero_source, one_source, target):
        semaphore = self.semaphores.at[self.used]
        self.used += 1

        @pl.when(first)
        def _():
            pltpu.make_async_copy(zero_source, target, semaphore).start()

        @pl.when(jnp.logical_not(first))
        def _():
            pltpu.make_async_copy(one_source, target, semaphore).start()

        return pltpu.make_async_copy(zero_source, target, semaphore)


def rows_from(position, distance, row_count, count):
    source = lax.rem(position - distance + count, count)
    return pl.ds(pl.multiple_of(source * row_count, row_count), row_count)


def orthonormalize(power_ref, q_ref, gram_ref):
    bf16 = jnp.bfloat16
    width = gram_ref.shape[0]
    for start in range(0, power_ref.shape[1], width):
        span = slice(start, start + width)
        group = power_ref[:, span]
        if start > 0:
            along = product(q_ref[:, :start], group.astype(bf16), TN).astype(bf16)
            group = group - product(q_ref[:, :start], along, NN)
        group = (group * lax.rsqrt(jnp.sum(group * group, axis=0, keepdims=True))).astype(bf16)
        gram_ref[...] = product(group, group, TN)
        invert_factor(gram_ref)
        inverse = split_cat(gram_ref[...], "hl", 1)
        q_ref[:, span] = product(jnp.concatenate([group, group], axis=1), inverse, NT).astype(bf16)


def share_kernel(symmetric, place_ref, factor_ref, basis_ref, early_ref, share_ref, late_ref):
    row_count, order = factor_ref.shape
    count = order // row_count
    width = order // 4
    bf16 = jnp.bfloat16
    shared = share_ref.shape[1] - width
    early_ref[...] = basis_ref[:, :width].astype(bf16)
    share_ref[:, shared:] = basis_ref[:, width : 2 * width].astype(bf16)
    late_ref[...] = basis_ref[:, 2 * width :].astype(bf16)
    if not symmetric:
        share_ref[:, :shared] = factor_ref[...].astype(bf16)
        return
    half = row_count // 2
    for r in range(count):

        @pl.when(place_ref[1] == r)
        def _():
            for offset in range(count // 2):
                start = (r + offset) % count * row_count
                share_ref[:, offset * row_count : (offset + 1) * row_count] = factor_ref[
                    :, start : start + row_count
                ].astype(bf16)
            start = (r + count // 2) % count * row_count
            if r < count // 2:
                last = factor_ref[:, start : start + half]
            else:
                last = factor_ref[half:, start : start + row_count].T
            share_ref[:, count // 2 * row_count : shared] = last.astype(bf16)


def gather_shares(place, factor_rows, basis_rows, symmetric):
    row_count, order = factor_rows.shape
    shared = order // 2 + row_count // 2 if symmetric else order
    vmem = pl.BlockSpec(memory_space=pltpu.VMEM)
    return pl.pallas_call(
        functools.partial(share_kernel, symmetric),
        out_shape=tuple(
            jax.ShapeDtypeStruct((row_count, columns), jnp.bfloat16)
            for columns in (order // 4, shared + order // 4, order // 2)
        ),
        in_specs=[SMEM, vmem, vmem],
        out_specs=(vmem,) * 3,
        cost_estimate=pl.CostEstimate(flops=0, bytes_accessed=3 * 2**20, transcendentals=0),
        compiler_params=pltpu.CompilerParams(vmem_limit_bytes=VMEM_GRANT),
        name="gather_shares",
    )(place, factor_rows, basis_rows)


def first_kernel(half_steps, count, place_ref, gathered_hbm, rows_hbm, *refs):
    own, other, basis = refs[:count], refs[count : 2 * count], refs[2 * count : 3 * count]
    whole_hbm, new_rows_hbm, q_hbm = refs[3 * count : 3 * count + 3]
    block, old, columns, rows, whole, new_rows, power, q, gram, semaphores = refs[3 * count + 3 :]
    row_count, order = rows.shape
    half_width = order // 2
    width = order // 4
    shared = old.shape[1]
    first = place_ref[0] == 0
    copies = Copies(semaphores)
    waits, late = [], []
    for k in range(count):
        span = rows_from(place_ref[1], k, row_count, count)
        waits.append(copies.start_either(first, own[k], other[k], block.at[span, pl.ds(0, half_width)]))
        waits.append(copies.start_either(first, other[k], own[k], block.at[span, pl.ds(half_width, half_width)]))
    waits.append(copies.start(gathered_hbm.at[:, pl.ds(0, shared)], old))
    waits.append(copies.start(rows_hbm, rows))
    late.append(copies.start(gathered_hbm.at[:, pl.ds(shared, width)], columns.at[:, pl.ds(width, width)]))
    for k in range(count):
        span = rows_from(place_ref[1], k, row_count, count)
        late.append(copies.start(basis[k], columns.at[span, pl.ds(0, width)]))
    for copy in waits:
        copy.wait()

    def old_block(r, c):
        offset = (c - r) % count
        row = slice(r * row_count, (r + 1) * row_count)
        if half_steps is None:
            return old[row, c * row_count : (c + 1) * row_count].astype(jnp.float32)
        if offset < half_steps:
            return old[row, offset * row_count : (offset + 1) * row_count].astype(jnp.float32)
        if offset > half_steps or r >= half_steps:
            return old_block(c, r).T
        mirror = slice(c * row_count, (c + 1) * row_count)
        part = slice(half_steps * row_count, half_steps * row_count + row_count // 2)
        return jnp.concatenate([old[row, part], old[mirror, part]], axis=1).astype(jnp.float32)

    @pl.when(first)
    def _():
        for start in range(0, order, width):
            power[start : start + width, :] = product(block[start : start + width, :], block[...], NT)

    @pl.when(jnp.logical_not(first))
    def _():
        for start in range(0, order, width):
            power[start : start + width, :] = product(block[:, start : start + width], block[...], TN)

    here = rows_from(place_ref[1], 0, row_count, count)
    new_rows[...] = 0.95 * rows[...] + 0.05 * power[here, :]
    for r in range(count):
        row = slice(r * row_count, (r + 1) * row_count)
        rest = jnp.concatenate([old_block(r, c) for c in range(count)], axis=1)
        whole[row, :] = (0.95 * rest + 0.05 * power[row, :]).astype(jnp.bfloat16)
    outputs = [copies.start(new_rows, new_rows_hbm), copies.start(whole, whole_hbm)]
    for copy in late:
        copy.wait()
    power[:, :half_width] = product(whole[...], columns[...], NN)
    orthonormalize(power.at[:, pl.ds(0, half_width)], q, gram)
    outputs.append(copies.start(q, q_hbm))
    for copy in outputs:
        copy.wait()


def first_half(place, own, other, basis, gathered, rows, half_steps):
    row_count, order = rows.shape
    count = len(own)
    half = order // 2
    bf16, f32 = jnp.bfloat16, jnp.float32
    shape, vmem = jax.ShapeDtypeStruct, pltpu.VMEM
    return kernel_call(
        functools.partial(first_kernel, half_steps, count),
        "first_half",
        (shape((order, order), bf16), shape(rows.shape, f32), shape((order, half), bf16)),
        [
            vmem((order, order), bf16),
            vmem((order, gathered.shape[1] - order // 4), bf16),
            vmem((order, half), bf16),
            vmem(rows.shape, f32),
            vmem((order, order), bf16),
            vmem(rows.shape, f32),
            vmem((order, order), f32),
            vmem((order, half), bf16),
            vmem((half // 2, half // 2), f32),
            pltpu.SemaphoreType.DMA((3 * count + 6,)),
        ],
        6 * order**3,
        (place, gathered, rows, *own, *other, *basis),
    )


def second_kernel(count, place_ref, whole_hbm, before_hbm, *refs):
    basis, (q_hbm, rows_hbm) = refs[:count], refs[count : count + 2]
    whole, before, columns, power, q, gram, semaphores = refs[count + 2 :]
    order, half = before.shape
    row_count = order // count
    bf16 = jnp.bfloat16
    here = rows_from(place_ref[1], 0, row_count, count)
    copies = Copies(semaphores)
    waits = [copies.start(whole_hbm, whole)]
    for k in range(count):
        waits.append(copies.start(basis[k], columns.at[rows_from(place_ref[1], k, row_count, count), :]))
    last = copies.start(before_hbm, before)
    for copy in waits:
        copy.wait()
    power[...] = product(whole[...], columns[...], NN)
    last.wait()
    outputs = [copies.start(before.at[here, :], rows_hbm.at[:, pl.ds(0, half)])]
    along = product(before[...], power[...].astype(bf16), TN)
    power[...] = power[...] - product(before[...], along.astype(bf16), NN)
    orthonormalize(power, q, gram)
    outputs.append(copies.start(q, q_hbm))
    outputs.append(copies.start(q.at[here, :], rows_hbm.at[:, pl.ds(half, half)]))
    for copy in outputs:
        copy.wait()


def second_half(place, basis, whole, before):
    order, half = before.shape
    row_count = order // len(basis)
    bf16, f32 = jnp.bfloat16, jnp.float32
    shape, vmem = jax.ShapeDtypeStruct, pltpu.VMEM
    return kernel_call(
        functools.partial(second_kernel, len(basis)),
        "second_half",
        (shape((order, half), bf16), shape((row_count, order), bf16)),
        [
            vmem((order, order), bf16),
            vmem((order, half), bf16),
            vmem((order, half), bf16),
            vmem((order, half), f32),
            vmem((order, half), bf16),
            vmem((half // 2, half // 2), f32),
            pltpu.SemaphoreType.DMA((len(basis) + 5,)),
        ],
        4 * order**3,
        (place, whole, before, *basis),
    )


def moment_kernel(count, place_ref, *refs):
    own, other, own_pieces, other_pieces = refs[:2], refs[2:4], refs[4 : 4 + count], refs[4 + count : 4 + 2 * count]
    moments_hbm, first_hbm, second_hbm = refs[4 + 2 * count : 7 + 2 * count]
    weighted_hbm, first_out, second_out = refs[7 + 2 * count : 10 + 2 * count]
    left, right, block, moments, first_rows, second_rows, mixed, rotated, normal, weighted, semaphores = refs[
        10 + 2 * count :
    ]
    row_count, half_width = first_rows.shape
    order = left.shape[0]
    f32, bf16 = jnp.float32, jnp.bfloat16
    first = place_ref[0] == 0
    here = rows_from(place_ref[1], 0, row_count, count)
    upper, lower = pl.ds(0, half_width), pl.ds(half_width, half_width)
    copies = Copies(semaphores)
    early = [copies.start_either(first, other[0], own[1], right)]
    for k in range(count):
        span = rows_from(place_ref[1], k, row_count, count)
        early.append(copies.start_either(first, own_pieces[k], other_pieces[k], block.at[span, upper]))
        early.append(copies.start_either(first, other_pieces[k], own_pieces[k], block.at[span, lower]))
    late = [
        copies.start_either(first, own[0], other[0], left.at[:, upper]),
        copies.start_either(first, own[1], other[1], left.at[:, lower]),
        copies.start(moments_hbm, moments),
        copies.start(first_hbm, first_rows),
        copies.start(second_hbm, second_rows),
    ]
    for copy in early:
        copy.wait()
    mixed[...] = product(block[...], right[...], NN).astype(bf16)
    for copy in late:
        copy.wait()
    total = jnp.zeros(weighted.shape, f32)
    width = order // 4
    for start in range(0, order, width):
        span = slice(start, start + width)
        turn = product(left[:, span], mixed[...], TN)
        rotated[span, :] = turn
        new_first = 0.95 * moments[span, :half_width].astype(f32) + 0.05 * turn
        new_second = 0.95 * moments[span, half_width:].astype(f32) + 0.05 * turn * turn
        normal[span, :] = (new_first / (jnp.sqrt(new_second) + 1e-08)).astype(bf16)
        total = total + product(left[here, span], normal[span, :], NN)
    weighted[...] = total.astype(bf16)
    outputs = [copies.start(weighted, weighted_hbm)]
    turn = rotated[here, :]
    first_rows[...] = 0.95 * first_rows[...] + 0.05 * turn
    second_rows[...] = 0.95 * second_rows[...] + 0.05 * turn * turn
    outputs += [copies.start(first_rows, first_out), copies.start(second_rows, second_out)]
    for copy in outputs:
        copy.wait()


def moment_step(place, own, other, own_pieces, other_pieces, moments, first, second):
    order = own[0].shape[0]
    half = first.shape[1]
    count = len(own_pieces)
    f32, bf16 = jnp.float32, jnp.bfloat16
    shape, vmem = jax.ShapeDtypeStruct, pltpu.VMEM
    return kernel_call(
        functools.partial(moment_kernel, count),
        "moment_step",
        (shape(first.shape, bf16), shape(first.shape, f32), shape(first.shape, f32)),
        [
            vmem((order, order), bf16),
            vmem((order, half), bf16),
            vmem((order, order), bf16),
            vmem((order, order), bf16),
            vmem(first.shape, f32),
            vmem(first.shape, f32),
            vmem((order, half), bf16),
            vmem((order, half), f32),
            vmem((order, half), bf16),
            vmem(first.shape, bf16),
            pltpu.SemaphoreType.DMA((2 * count + 9,)),
        ],
        4 * order * order * half,
        (place, *own, *other, *own_pieces, *other_pieces, moments, first, second),
    )


def direction_kernel(place_ref, *refs):
    own, other, (mine_hbm, theirs_hbm, out_hbm) = refs[:2], refs[2:4], refs[4:7]
    near, far, mine, theirs, out, semaphores = refs[7:]
    half = near.shape[0]
    upper, lower = pl.ds(0, half), pl.ds(half, half)
    first = place_ref[0] == 0
    copies = Copies(semaphores)
    waits = [
        copies.start(mine_hbm, mine),
        copies.start(theirs_hbm, theirs),
        copies.start_either(first, other[0].at[upper, :], own[1].at[lower, :], near),
        copies.start_either(first, other[1].at[upper, :], own[0].at[lower, :], far),
    ]
    for copy in waits:
        copy.wait()
    out[...] = (product(mine[...], near[...], NT) + product(theirs[...], far[...], NT)).astype(out.dtype)
    copies.start(out, out_hbm).wait()


def direction_step(place, own, other, mine, theirs):
    half = mine.shape[1]
    vmem = pltpu.VMEM
    square, rows = vmem((half, half), mine.dtype), vmem(mine.shape, mine.dtype)
    return kernel_call(
        direction_kernel,
        "direction_step",
        jax.ShapeDtypeStruct(mine.shape, mine.dtype),
        [square, square, rows, rows, rows, pltpu.SemaphoreType.DMA((5,))],
        4 * mine.shape[0] * half * half,
        (place, *own, *other, mine, theirs),
    )


def exchanged(block, axis, partner_of):
    count = lax.axis_size(axis)
    return lax.ppermute(block, axis, [(i, partner_of(i)) for i in range(count)])


def sibling(block):
    return exchanged(block, "dp", lambda i: i ^ 1)


def rounded_sum(x, y):
    return (x.astype(jnp.float32) + y.astype(jnp.float32)).astype(jnp.bfloat16)


def reversed_bits(value, bits):
    return sum(((value >> k) & 1) << (bits - 1 - k) for k in range(bits))


def pair_terms(partial_rows, half_width):
    side = lax.axis_index("dp") % 2
    blocks = lax.axis_size("dp") // 2
    bits = blocks.bit_length() - 1
    row_blocks, _, columns = partial_rows.shape
    halves = [
        partial_rows[rb, :, start : start + half_width]
        for rb in range(row_blocks)
        for start in range(0, columns, half_width)
    ]
    lows, highs = halves[0::2], halves[1::2]
    turned = [reversed_bits(k, bits) for k in range(blocks)]
    keep = jnp.stack([jnp.where(side == 0, lows[k], highs[turned[k]]) for k in range(blocks)])
    send = jnp.stack([jnp.where(side == 0, highs[turned[k]], lows[k]) for k in range(blocks)])
    return send, keep


def reduced_half_block(held):
    position = lax.axis_index("dp")
    side = position % 2
    bits = held.shape[0].bit_length() - 1
    for step in range(bits):
        low_bit, high_bit = 1 + step, bits - step
        mine = jnp.where(side == 0, position >> high_bit, position >> low_bit) & 1
        middle = held.shape[0] // 2
        keep = jnp.where(mine == 0, held[:middle], held[middle:])
        send = jnp.where(mine == 0, held[middle:], held[:middle])
        arrived = exchanged(send, "dp", lambda i: i ^ (1 << (low_bit if i % 2 else high_bit)))
        held = rounded_sum(keep, arrived)
    return held[0]


def pieces_by_distance(shard, axis):
    count = lax.axis_size(axis)
    return [shard] + [
        lax.ppermute(shard, axis, [(i, (i + distance) % count) for i in range(count)]) for distance in range(1, count)
    ]


def body(grad_partial, factors, bases, first_moment, second_moment):
    row_count, block_width = factors.shape[1:]
    half_width = block_width // 2
    side = lax.axis_index("dp") % 2
    position, count = lax.axis_index("fsdp"), lax.axis_size("fsdp")
    place = jnp.stack([side, position]).astype(jnp.int32)
    bf16 = jnp.bfloat16

    symmetric = row_count % 256 == 0 and count % 2 == 0
    early, share, late = gather_shares(place, factors[0], bases[0], symmetric)
    first_pieces = pieces_by_distance(early, "fsdp")
    gathered = lax.all_gather(share, "fsdp", axis=0, tiled=True)
    send, keep = pair_terms(grad_partial[0], half_width)
    pair_sum, first_pieces[1] = lax.optimization_barrier((rounded_sum(keep, sibling(send)), first_pieces[1]))
    own_half, first_pieces = lax.optimization_barrier((reduced_half_block(pair_sum), first_pieces))
    own_pieces = pieces_by_distance(own_half, "fsdp")
    other_pieces = [sibling(piece) for piece in own_pieces]

    moments = jnp.concatenate([first_moment[0].astype(bf16), second_moment[0].astype(bf16)], axis=1)
    late, moments, own_pieces = lax.optimization_barrier((late, moments, own_pieces))
    late_pieces = pieces_by_distance(late, "fsdp")
    moments = lax.all_gather(moments, "fsdp", axis=0, tiled=True)

    factor_whole, new_factor_rows, first_q = first_half(
        place, own_pieces, other_pieces, first_pieces, gathered, factors[0], count // 2 if symmetric else None
    )
    first_other = sibling(first_q)
    second_q, new_rows = second_half(place, late_pieces, factor_whole, first_q)
    own, other = (first_q, second_q), (first_other, sibling(second_q))
    weighted, first_new, second_new = moment_step(
        place, own, other, own_pieces, other_pieces, moments, first_moment[0], second_moment[0]
    )
    direction = direction_step(place, own, other, weighted, sibling(weighted))
    return (new_factor_rows[None], new_rows[None], first_new[None], second_new[None], direction[None])


def solution(mesh):
    rows = P("dp", "fsdp", None)
    return jax.shard_map(
        body,
        mesh=mesh,
        in_specs=(P("dp", None, "fsdp", None), rows, rows, rows, rows),
        out_specs=(rows,) * 5,
        check_vma=False,
    )
```

```python
import functools

import jax
import jax.numpy as jnp
from jax import lax
from jax.experimental import pallas as pl
from jax.experimental.pallas import tpu as pltpu
from jax.sharding import PartitionSpec as P

TILE = 128
SUB = 8
VMEM_GRANT = 60 * 2**20


def splat_lane(x, lane):
    return jnp.broadcast_to(x[:, lane : lane + 1], x.shape)


def splat_row(x, row):
    return jnp.broadcast_to(x[row : row + 1, :], x.shape)


def reciprocal(x):
    guess = pl.reciprocal(x, approx=True)
    return guess * (2.0 - x * guess)


def tree_sum(terms):
    while len(terms) > 1:
        terms = [x + y for x, y in zip(terms[0::2], terms[1::2])]
    return terms[0]


def inverse_columns(columns, sub):
    held = list(columns)
    for p in range(0, SUB, 2):
        first, second = held[p], held[p + 1]
        a, b, c = splat_row(first, p), splat_row(second, p), splat_row(second, p + 1)
        inverse = reciprocal(a * c - b * b)
        at_first, at_second = sub == p, sub == p + 1
        left = jnp.where(at_first, -c, jnp.where(at_second, b, c * first - b * second))
        right = jnp.where(at_first, b, jnp.where(at_second, -a, a * second - b * first))
        for k in range(SUB):
            if k == p:
                held[k] = -left * inverse
            elif k == p + 1:
                held[k] = -right * inverse
            else:
                taken = left * splat_row(held[k], p) + right * splat_row(held[k], p + 1)
                held[k] = jnp.where(at_first | at_second, 0.0, held[k]) - taken * inverse
    return held


def scaled_rows(columns, rows, sub):
    columns = list(columns)
    for p in range(SUB):
        pivot = splat_row(columns[p], p)
        scale = lax.rsqrt(pivot)
        factor = jnp.where(sub > p, columns[p] * (scale * scale), 0.0)
        for k in range(p + 1, SUB):
            columns[k] = columns[k] - factor * splat_row(columns[k], p)
        rows = jnp.where(sub == p, rows * scale, rows - factor * splat_row(rows, p))
    return rows


def tile_inverse(tile):
    size = tile.shape[0]
    count = size // SUB
    lane = lax.broadcasted_iota(jnp.int32, (SUB, size), 1)
    sub = lax.broadcasted_iota(jnp.int32, (SUB, size), 0)
    groups = [tile[SUB * g : SUB * (g + 1), :] for g in range(count)]
    result = []
    for g in range(count):
        base = SUB * g
        in_block = (lane >= base) & (lane < base + SUB)
        pivots = [splat_lane(groups[g], base + k) for k in range(SUB)]
        inverse = inverse_columns(pivots, sub)
        one = jnp.where(lane == base + sub, 1.0, 0.0)
        own = jnp.where(in_block, one, groups[g])
        result.append(scaled_rows(pivots, jnp.where(lane < base, groups[g], one), sub))
        if g == count - 1:
            break
        applied = tree_sum([inverse[k] * splat_row(own, k) for k in range(SUB)])
        spread = [splat_row(applied, k) for k in range(SUB)]
        for h in range(g + 1, count):
            taken = tree_sum([splat_lane(groups[h], base + k) * spread[k] for k in range(SUB)])
            groups[h] = jnp.where(in_block, 0.0, groups[h]) - taken
    return jnp.concatenate(result, axis=0)


def split_cat(x, which, axis):
    hi = x.astype(jnp.bfloat16)
    lo = (x - hi.astype(jnp.float32)).astype(jnp.bfloat16)
    return jnp.concatenate([hi if w == "h" else lo for w in which], axis=axis)


def product(x, y, dims):
    return lax.dot_general(x, y, (dims, ((), ())), preferred_element_type=jnp.float32)


def product3(x, y, dims):
    (cx,), (cy,) = dims
    return product(split_cat(x, "hhl", cx), split_cat(y, "hlh", cy), dims)


NN, NT, TN = ((1,), (0,)), ((1,), (1,)), ((0,), (0,))


def invert_factor(ref):
    order = ref.shape[0]
    tiles = order // TILE
    lane = lax.broadcasted_iota(jnp.int32, (TILE, order), 1)
    row = lax.broadcasted_iota(jnp.int32, (TILE, order), 0)

    def step(j, carry):
        start = pl.multiple_of(j * TILE, TILE)
        rows = pl.ds(start, TILE)
        inverse = tile_inverse(ref[rows, rows])
        in_tile = (lane >= start) & (lane < start + TILE)
        whole = jnp.where(in_tile, jnp.where(lane - start == row, 1.0, 0.0), ref[rows, :])
        reduced = product3(inverse, whole, NN)
        ref[rows, :] = jnp.where(lane < start + TILE, reduced, 0.0)
        right = split_cat(reduced, "hlh", 0)

        def update(i, c):
            below = pl.ds(pl.multiple_of(i * TILE, TILE), TILE)
            left = product3(ref[below, rows], inverse, NT)
            kept = jnp.where(in_tile, 0.0, ref[below, :])
            ref[below, :] = kept - product(split_cat(left, "hhl", 1), right, NN)
            return c

        lax.fori_loop(j + 1, tiles, update, 0)
        return carry

    lax.fori_loop(0, tiles, step, 0)


HBM = pl.BlockSpec(memory_space=pl.ANY)
SMEM = pl.BlockSpec(memory_space=pltpu.SMEM)


def kernel_call(kernel, name, out_shape, scratch, flops, operands):
    return pl.pallas_call(
        kernel,
        out_shape=out_shape,
        in_specs=[SMEM] + [HBM] * (len(operands) - 1),
        out_specs=jax.tree.map(lambda _: HBM, out_shape),
        scratch_shapes=scratch,
        cost_estimate=pl.CostEstimate(flops=flops, bytes_accessed=16 * 2**20, transcendentals=0),
        compiler_params=pltpu.CompilerParams(vmem_limit_bytes=VMEM_GRANT),
        name=name,
    )(*operands)


class Copies:
    def __init__(self, semaphores):
        self.semaphores, self.used = semaphores, 0

    def start(self, source, target):
        copy = pltpu.make_async_copy(source, target, self.semaphores.at[self.used])
        self.used += 1
        copy.start()
        return copy

    def start_either(self, first, zero_source, one_source, target):
        semaphore = self.semaphores.at[self.used]
        self.used += 1

        @pl.when(first)
        def _():
            pltpu.make_async_copy(zero_source, target, semaphore).start()

        @pl.when(jnp.logical_not(first))
        def _():
            pltpu.make_async_copy(one_source, target, semaphore).start()

        return pltpu.make_async_copy(zero_source, target, semaphore)


def rows_from(position, distance, row_count, count):
    source = lax.rem(position - distance + count, count)
    return pl.ds(pl.multiple_of(source * row_count, row_count), row_count)


def orthonormalize(power_ref, q_ref, gram_ref):
    bf16 = jnp.bfloat16
    width = gram_ref.shape[0]
    for start in range(0, power_ref.shape[1], width):
        span = slice(start, start + width)
        group = power_ref[:, span]
        if start > 0:
            along = product(q_ref[:, :start], group.astype(bf16), TN).astype(bf16)
            group = group - product(q_ref[:, :start], along, NN)
        group = (group * lax.rsqrt(jnp.sum(group * group, axis=0, keepdims=True))).astype(bf16)
        gram_ref[...] = product(group, group, TN)
        invert_factor(gram_ref)
        inverse = split_cat(gram_ref[...], "hl", 1)
        q_ref[:, span] = product(jnp.concatenate([group, group], axis=1), inverse, NT).astype(bf16)


def share_kernel(symmetric, place_ref, factor_ref, basis_ref, early_ref, share_ref, late_ref):
    row_count, order = factor_ref.shape
    count = order // row_count
    width = order // 4
    bf16 = jnp.bfloat16
    shared = share_ref.shape[1] - width
    early_ref[...] = basis_ref[:, :width].astype(bf16)
    share_ref[:, shared:] = basis_ref[:, width : 2 * width].astype(bf16)
    late_ref[...] = basis_ref[:, 2 * width :].astype(bf16)
    if not symmetric:
        share_ref[:, :shared] = factor_ref[...].astype(bf16)
        return
    half = row_count // 2
    for r in range(count):

        @pl.when(place_ref[1] == r)
        def _():
            for offset in range(count // 2):
                start = (r + offset) % count * row_count
                share_ref[:, offset * row_count : (offset + 1) * row_count] = factor_ref[
                    :, start : start + row_count
                ].astype(bf16)
            start = (r + count // 2) % count * row_count
            if r < count // 2:
                last = factor_ref[:, start : start + half]
            else:
                last = factor_ref[half:, start : start + row_count].T
            share_ref[:, count // 2 * row_count : shared] = last.astype(bf16)


def gather_shares(place, factor_rows, basis_rows, symmetric):
    row_count, order = factor_rows.shape
    shared = order // 2 + row_count // 2 if symmetric else order
    vmem = pl.BlockSpec(memory_space=pltpu.VMEM)
    return pl.pallas_call(
        functools.partial(share_kernel, symmetric),
        out_shape=tuple(
            jax.ShapeDtypeStruct((row_count, columns), jnp.bfloat16)
            for columns in (order // 4, shared + order // 4, order // 2)
        ),
        in_specs=[SMEM, vmem, vmem],
        out_specs=(vmem,) * 3,
        cost_estimate=pl.CostEstimate(flops=0, bytes_accessed=3 * 2**20, transcendentals=0),
        compiler_params=pltpu.CompilerParams(vmem_limit_bytes=VMEM_GRANT),
        name="gather_shares",
    )(place, factor_rows, basis_rows)


def first_kernel(half_steps, count, place_ref, gathered_hbm, rows_hbm, *refs):
    own, other, basis = refs[:count], refs[count : 2 * count], refs[2 * count : 3 * count]
    whole_hbm, new_rows_hbm, q_hbm = refs[3 * count : 3 * count + 3]
    block, old, columns, rows, whole, new_rows, power, q, gram, semaphores = refs[3 * count + 3 :]
    row_count, order = rows.shape
    half_width = order // 2
    width = order // 4
    shared = old.shape[1]
    first = place_ref[0] == 0
    copies = Copies(semaphores)
    waits, late = [], []
    for k in range(count):
        span = rows_from(place_ref[1], k, row_count, count)
        waits.append(copies.start_either(first, own[k], other[k], block.at[span, pl.ds(0, half_width)]))
        waits.append(copies.start_either(first, other[k], own[k], block.at[span, pl.ds(half_width, half_width)]))
    waits.append(copies.start(gathered_hbm.at[:, pl.ds(0, shared)], old))
    waits.append(copies.start(rows_hbm, rows))
    late.append(copies.start(gathered_hbm.at[:, pl.ds(shared, width)], columns.at[:, pl.ds(width, width)]))
    for k in range(count):
        span = rows_from(place_ref[1], k, row_count, count)
        late.append(copies.start(basis[k], columns.at[span, pl.ds(0, width)]))
    for copy in waits:
        copy.wait()

    def old_block(r, c):
        offset = (c - r) % count
        row = slice(r * row_count, (r + 1) * row_count)
        if half_steps is None:
            return old[row, c * row_count : (c + 1) * row_count].astype(jnp.float32)
        if offset < half_steps:
            return old[row, offset * row_count : (offset + 1) * row_count].astype(jnp.float32)
        if offset > half_steps or r >= half_steps:
            return old_block(c, r).T
        mirror = slice(c * row_count, (c + 1) * row_count)
        part = slice(half_steps * row_count, half_steps * row_count + row_count // 2)
        return jnp.concatenate([old[row, part], old[mirror, part]], axis=1).astype(jnp.float32)

    @pl.when(first)
    def _():
        for start in range(0, order, width):
            power[start : start + width, :] = product(block[start : start + width, :], block[...], NT)

    @pl.when(jnp.logical_not(first))
    def _():
        for start in range(0, order, width):
            power[start : start + width, :] = product(block[:, start : start + width], block[...], TN)

    here = rows_from(place_ref[1], 0, row_count, count)
    new_rows[...] = 0.95 * rows[...] + 0.05 * power[here, :]
    for r in range(count):
        row = slice(r * row_count, (r + 1) * row_count)
        rest = jnp.concatenate([old_block(r, c) for c in range(count)], axis=1)
        whole[row, :] = (0.95 * rest + 0.05 * power[row, :]).astype(jnp.bfloat16)
    outputs = [copies.start(new_rows, new_rows_hbm), copies.start(whole, whole_hbm)]
    for copy in late:
        copy.wait()
    power[:, :half_width] = product(whole[...], columns[...], NN)
    orthonormalize(power.at[:, pl.ds(0, half_width)], q, gram)
    outputs.append(copies.start(q, q_hbm))
    for copy in outputs:
        copy.wait()


def first_half(place, own, other, basis, gathered, rows, half_steps):
    row_count, order = rows.shape
    count = len(own)
    half = order // 2
    bf16, f32 = jnp.bfloat16, jnp.float32
    shape, vmem = jax.ShapeDtypeStruct, pltpu.VMEM
    return kernel_call(
        functools.partial(first_kernel, half_steps, count),
        "first_half",
        (shape((order, order), bf16), shape(rows.shape, f32), shape((order, half), bf16)),
        [
            vmem((order, order), bf16),
            vmem((order, gathered.shape[1] - order // 4), bf16),
            vmem((order, half), bf16),
            vmem(rows.shape, f32),
            vmem((order, order), bf16),
            vmem(rows.shape, f32),
            vmem((order, order), f32),
            vmem((order, half), bf16),
            vmem((half // 2, half // 2), f32),
            pltpu.SemaphoreType.DMA((3 * count + 6,)),
        ],
        6 * order**3,
        (place, gathered, rows, *own, *other, *basis),
    )


def second_kernel(row_count, place_ref, columns_hbm, whole_hbm, before_hbm, q_hbm, rows_hbm, *refs):
    whole, before, columns, power, q, gram, semaphores = refs
    order, half = before.shape
    bf16 = jnp.bfloat16
    here = rows_from(place_ref[1], 0, row_count, order // row_count)
    copies = Copies(semaphores)
    waits = [copies.start(whole_hbm, whole), copies.start(columns_hbm, columns)]
    last = copies.start(before_hbm, before)
    for copy in waits:
        copy.wait()
    power[...] = product(whole[...], columns[...], NN)
    last.wait()
    outputs = [copies.start(before.at[here, :], rows_hbm.at[:, pl.ds(0, half)])]
    along = product(before[...], power[...].astype(bf16), TN)
    power[...] = power[...] - product(before[...], along.astype(bf16), NN)
    orthonormalize(power, q, gram)
    outputs.append(copies.start(q, q_hbm))
    outputs.append(copies.start(q.at[here, :], rows_hbm.at[:, pl.ds(half, half)]))
    for copy in outputs:
        copy.wait()


def second_half(place, columns, whole, before, row_count):
    order, half = before.shape
    bf16, f32 = jnp.bfloat16, jnp.float32
    shape, vmem = jax.ShapeDtypeStruct, pltpu.VMEM
    return kernel_call(
        functools.partial(second_kernel, row_count),
        "second_half",
        (shape((order, half), bf16), shape((row_count, order), bf16)),
        [
            vmem((order, order), bf16),
            vmem((order, half), bf16),
            vmem((order, half), bf16),
            vmem((order, half), f32),
            vmem((order, half), bf16),
            vmem((half // 2, half // 2), f32),
            pltpu.SemaphoreType.DMA((6,)),
        ],
        4 * order**3,
        (place, columns, whole, before),
    )


def moment_kernel(count, place_ref, *refs):
    own, other, own_pieces, other_pieces = refs[:2], refs[2:4], refs[4 : 4 + count], refs[4 + count : 4 + 2 * count]
    moments_hbm, first_hbm, second_hbm = refs[4 + 2 * count : 7 + 2 * count]
    weighted_hbm, first_out, second_out = refs[7 + 2 * count : 10 + 2 * count]
    left, right, block, moments, first_rows, second_rows, mixed, rotated, normal, weighted, semaphores = refs[
        10 + 2 * count :
    ]
    row_count, half_width = first_rows.shape
    order = left.shape[0]
    f32, bf16 = jnp.float32, jnp.bfloat16
    first = place_ref[0] == 0
    here = rows_from(place_ref[1], 0, row_count, count)
    upper, lower = pl.ds(0, half_width), pl.ds(half_width, half_width)
    copies = Copies(semaphores)
    early = [copies.start_either(first, other[0], own[1], right)]
    for k in range(count):
        span = rows_from(place_ref[1], k, row_count, count)
        early.append(copies.start_either(first, own_pieces[k], other_pieces[k], block.at[span, upper]))
        early.append(copies.start_either(first, other_pieces[k], own_pieces[k], block.at[span, lower]))
    late = [
        copies.start_either(first, own[0], other[0], left.at[:, upper]),
        copies.start_either(first, own[1], other[1], left.at[:, lower]),
        copies.start(moments_hbm, moments),
        copies.start(first_hbm, first_rows),
        copies.start(second_hbm, second_rows),
    ]
    for copy in early:
        copy.wait()
    mixed[...] = product(block[...], right[...], NN).astype(bf16)
    for copy in late:
        copy.wait()
    total = jnp.zeros(weighted.shape, f32)
    width = order // 4
    for start in range(0, order, width):
        span = slice(start, start + width)
        turn = product(left[:, span], mixed[...], TN)
        rotated[span, :] = turn
        new_first = 0.95 * moments[span, :half_width].astype(f32) + 0.05 * turn
        new_second = 0.95 * moments[span, half_width:].astype(f32) + 0.05 * turn * turn
        normal[span, :] = (new_first / (jnp.sqrt(new_second) + 1e-08)).astype(bf16)
        total = total + product(left[here, span], normal[span, :], NN)
    weighted[...] = total.astype(bf16)
    outputs = [copies.start(weighted, weighted_hbm)]
    turn = rotated[here, :]
    first_rows[...] = 0.95 * first_rows[...] + 0.05 * turn
    second_rows[...] = 0.95 * second_rows[...] + 0.05 * turn * turn
    outputs += [copies.start(first_rows, first_out), copies.start(second_rows, second_out)]
    for copy in outputs:
        copy.wait()


def moment_step(place, own, other, own_pieces, other_pieces, moments, first, second):
    order = own[0].shape[0]
    half = first.shape[1]
    count = len(own_pieces)
    f32, bf16 = jnp.float32, jnp.bfloat16
    shape, vmem = jax.ShapeDtypeStruct, pltpu.VMEM
    return kernel_call(
        functools.partial(moment_kernel, count),
        "moment_step",
        (shape(first.shape, bf16), shape(first.shape, f32), shape(first.shape, f32)),
        [
            vmem((order, order), bf16),
            vmem((order, half), bf16),
            vmem((order, order), bf16),
            vmem((order, order), bf16),
            vmem(first.shape, f32),
            vmem(first.shape, f32),
            vmem((order, half), bf16),
            vmem((order, half), f32),
            vmem((order, half), bf16),
            vmem(first.shape, bf16),
            pltpu.SemaphoreType.DMA((2 * count + 9,)),
        ],
        4 * order * order * half,
        (place, *own, *other, *own_pieces, *other_pieces, moments, first, second),
    )


def direction_kernel(place_ref, *refs):
    own, other, (mine_hbm, theirs_hbm, out_hbm) = refs[:2], refs[2:4], refs[4:7]
    near, far, mine, theirs, out, semaphores = refs[7:]
    half = near.shape[0]
    upper, lower = pl.ds(0, half), pl.ds(half, half)
    first = place_ref[0] == 0
    copies = Copies(semaphores)
    waits = [
        copies.start(mine_hbm, mine),
        copies.start(theirs_hbm, theirs),
        copies.start_either(first, other[0].at[upper, :], own[1].at[lower, :], near),
        copies.start_either(first, other[1].at[upper, :], own[0].at[lower, :], far),
    ]
    for copy in waits:
        copy.wait()
    out[...] = (product(mine[...], near[...], NT) + product(theirs[...], far[...], NT)).astype(out.dtype)
    copies.start(out, out_hbm).wait()


def direction_step(place, own, other, mine, theirs):
    half = mine.shape[1]
    vmem = pltpu.VMEM
    square, rows = vmem((half, half), mine.dtype), vmem(mine.shape, mine.dtype)
    return kernel_call(
        direction_kernel,
        "direction_step",
        jax.ShapeDtypeStruct(mine.shape, mine.dtype),
        [square, square, rows, rows, rows, pltpu.SemaphoreType.DMA((5,))],
        4 * mine.shape[0] * half * half,
        (place, *own, *other, mine, theirs),
    )


def exchanged(block, axis, partner_of):
    count = lax.axis_size(axis)
    return lax.ppermute(block, axis, [(i, partner_of(i)) for i in range(count)])


def sibling(block):
    return exchanged(block, "dp", lambda i: i ^ 1)


def rounded_sum(x, y):
    return (x.astype(jnp.float32) + y.astype(jnp.float32)).astype(jnp.bfloat16)


def reversed_bits(value, bits):
    return sum(((value >> k) & 1) << (bits - 1 - k) for k in range(bits))


def pair_terms(partial_rows, half_width):
    side = lax.axis_index("dp") % 2
    blocks = lax.axis_size("dp") // 2
    bits = blocks.bit_length() - 1
    row_blocks, _, columns = partial_rows.shape
    halves = [
        partial_rows[rb, :, start : start + half_width]
        for rb in range(row_blocks)
        for start in range(0, columns, half_width)
    ]
    lows, highs = halves[0::2], halves[1::2]
    turned = [reversed_bits(k, bits) for k in range(blocks)]
    keep = jnp.stack([jnp.where(side == 0, lows[k], highs[turned[k]]) for k in range(blocks)])
    send = jnp.stack([jnp.where(side == 0, highs[turned[k]], lows[k]) for k in range(blocks)])
    return send, keep


def reduced_half_block(held, ahead):
    position = lax.axis_index("dp")
    side = position % 2
    bits = held.shape[0].bit_length() - 1
    for step in range(bits):
        low_bit, high_bit = 1 + step, bits - step
        mine = jnp.where(side == 0, position >> high_bit, position >> low_bit) & 1
        middle = held.shape[0] // 2
        keep = jnp.where(mine == 0, held[:middle], held[middle:])
        send = jnp.where(mine == 0, held[middle:], held[:middle])
        if step == 0:
            send, ahead = lax.optimization_barrier((send, ahead))
        arrived = exchanged(send, "dp", lambda i: i ^ (1 << (low_bit if i % 2 else high_bit)))
        held = rounded_sum(keep, arrived)
    return held[0], ahead


def pieces_by_distance(shard, axis):
    count = lax.axis_size(axis)
    return [shard] + [
        lax.ppermute(shard, axis, [(i, (i + distance) % count) for i in range(count)]) for distance in range(1, count)
    ]


def body(grad_partial, factors, bases, first_moment, second_moment):
    row_count, block_width = factors.shape[1:]
    half_width = block_width // 2
    side = lax.axis_index("dp") % 2
    position, count = lax.axis_index("fsdp"), lax.axis_size("fsdp")
    place = jnp.stack([side, position]).astype(jnp.int32)
    bf16 = jnp.bfloat16

    symmetric = row_count % 256 == 0 and count % 2 == 0
    early, share, late = gather_shares(place, factors[0], bases[0], symmetric)
    first_pieces = pieces_by_distance(early, "fsdp")
    gathered = lax.all_gather(share, "fsdp", axis=0, tiled=True)
    late = lax.all_gather(late, "fsdp", axis=0, tiled=True)
    send, keep = pair_terms(grad_partial[0], half_width)
    pair_sum = rounded_sum(keep, sibling(send))
    own_half, first_pieces = reduced_half_block(pair_sum, first_pieces)
    moments = jnp.concatenate([first_moment[0].astype(bf16), second_moment[0].astype(bf16)], axis=1)
    moments, own_half = lax.optimization_barrier((moments, own_half))
    moments = lax.all_gather(moments, "fsdp", axis=0, tiled=True)
    own_pieces = pieces_by_distance(own_half, "fsdp")
    other_pieces = [sibling(piece) for piece in own_pieces]

    factor_whole, new_factor_rows, first_q = first_half(
        place, own_pieces, other_pieces, first_pieces, gathered, factors[0], count // 2 if symmetric else None
    )
    first_other = sibling(first_q)
    second_q, new_rows = second_half(place, late, factor_whole, first_q, row_count)
    own, other = (first_q, second_q), (first_other, sibling(second_q))
    weighted, first_new, second_new = moment_step(
        place, own, other, own_pieces, other_pieces, moments, first_moment[0], second_moment[0]
    )
    direction = direction_step(place, own, other, weighted, sibling(weighted))
    return (new_factor_rows[None], new_rows[None], first_new[None], second_new[None], direction[None])


def solution(mesh):
    rows = P("dp", "fsdp", None)
    return jax.shard_map(
        body,
        mesh=mesh,
        in_specs=(P("dp", None, "fsdp", None), rows, rows, rows, rows),
        out_specs=(rows,) * 5,
        check_vma=False,
    )
```

```python
import functools

import jax
import jax.numpy as jnp
from jax import lax
from jax.experimental import pallas as pl
from jax.experimental.pallas import tpu as pltpu
from jax.sharding import PartitionSpec as P

TILE = 128
SUB = 8
VMEM_GRANT = 60 * 2**20


def splat_lane(x, lane):
    return jnp.broadcast_to(x[:, lane : lane + 1], x.shape)


def splat_row(x, row):
    return jnp.broadcast_to(x[row : row + 1, :], x.shape)


def reciprocal(x):
    guess = pl.reciprocal(x, approx=True)
    return guess * (2.0 - x * guess)


def tree_sum(terms):
    while len(terms) > 1:
        terms = [x + y for x, y in zip(terms[0::2], terms[1::2])]
    return terms[0]


def inverse_columns(columns, sub):
    held = list(columns)
    for p in range(0, SUB, 2):
        first, second = held[p], held[p + 1]
        a, b, c = splat_row(first, p), splat_row(second, p), splat_row(second, p + 1)
        inverse = reciprocal(a * c - b * b)
        at_first, at_second = sub == p, sub == p + 1
        left = jnp.where(at_first, -c, jnp.where(at_second, b, c * first - b * second))
        right = jnp.where(at_first, b, jnp.where(at_second, -a, a * second - b * first))
        for k in range(SUB):
            if k == p:
                held[k] = -left * inverse
            elif k == p + 1:
                held[k] = -right * inverse
            else:
                taken = left * splat_row(held[k], p) + right * splat_row(held[k], p + 1)
                held[k] = jnp.where(at_first | at_second, 0.0, held[k]) - taken * inverse
    return held


def scaled_rows(columns, rows, sub):
    columns = list(columns)
    for p in range(SUB):
        pivot = splat_row(columns[p], p)
        scale = lax.rsqrt(pivot)
        factor = jnp.where(sub > p, columns[p] * (scale * scale), 0.0)
        for k in range(p + 1, SUB):
            columns[k] = columns[k] - factor * splat_row(columns[k], p)
        rows = jnp.where(sub == p, rows * scale, rows - factor * splat_row(rows, p))
    return rows


def tile_inverse(tile):
    size = tile.shape[0]
    count = size // SUB
    lane = lax.broadcasted_iota(jnp.int32, (SUB, size), 1)
    sub = lax.broadcasted_iota(jnp.int32, (SUB, size), 0)
    groups = [tile[SUB * g : SUB * (g + 1), :] for g in range(count)]
    result = []
    for g in range(count):
        base = SUB * g
        in_block = (lane >= base) & (lane < base + SUB)
        pivots = [splat_lane(groups[g], base + k) for k in range(SUB)]
        inverse = inverse_columns(pivots, sub)
        one = jnp.where(lane == base + sub, 1.0, 0.0)
        own = jnp.where(in_block, one, groups[g])
        result.append(scaled_rows(pivots, jnp.where(lane < base, groups[g], one), sub))
        if g == count - 1:
            break
        applied = tree_sum([inverse[k] * splat_row(own, k) for k in range(SUB)])
        spread = [splat_row(applied, k) for k in range(SUB)]
        for h in range(g + 1, count):
            taken = tree_sum([splat_lane(groups[h], base + k) * spread[k] for k in range(SUB)])
            groups[h] = jnp.where(in_block, 0.0, groups[h]) - taken
    return jnp.concatenate(result, axis=0)


def split_cat(x, which, axis):
    hi = x.astype(jnp.bfloat16)
    lo = (x - hi.astype(jnp.float32)).astype(jnp.bfloat16)
    return jnp.concatenate([hi if w == "h" else lo for w in which], axis=axis)


def product(x, y, dims):
    return lax.dot_general(x, y, (dims, ((), ())), preferred_element_type=jnp.float32)


def product3(x, y, dims):
    (cx,), (cy,) = dims
    return product(split_cat(x, "hhl", cx), split_cat(y, "hlh", cy), dims)


NN, NT, TN = ((1,), (0,)), ((1,), (1,)), ((0,), (0,))


def invert_factor(ref):
    order = ref.shape[0]
    tiles = order // TILE
    lane = lax.broadcasted_iota(jnp.int32, (TILE, order), 1)
    row = lax.broadcasted_iota(jnp.int32, (TILE, order), 0)

    def step(j, carry):
        start = pl.multiple_of(j * TILE, TILE)
        rows = pl.ds(start, TILE)
        inverse = tile_inverse(ref[rows, rows])
        in_tile = (lane >= start) & (lane < start + TILE)
        whole = jnp.where(in_tile, jnp.where(lane - start == row, 1.0, 0.0), ref[rows, :])
        reduced = product3(inverse, whole, NN)
        ref[rows, :] = jnp.where(lane < start + TILE, reduced, 0.0)
        right = split_cat(reduced, "hlh", 0)

        def update(i, c):
            below = pl.ds(pl.multiple_of(i * TILE, TILE), TILE)
            left = product3(ref[below, rows], inverse, NT)
            kept = jnp.where(in_tile, 0.0, ref[below, :])
            ref[below, :] = kept - product(split_cat(left, "hhl", 1), right, NN)
            return c

        lax.fori_loop(j + 1, tiles, update, 0)
        return carry

    lax.fori_loop(0, tiles, step, 0)


HBM = pl.BlockSpec(memory_space=pl.ANY)
SMEM = pl.BlockSpec(memory_space=pltpu.SMEM)


def kernel_call(kernel, name, out_shape, scratch, flops, operands):
    return pl.pallas_call(
        kernel,
        out_shape=out_shape,
        in_specs=[SMEM] + [HBM] * (len(operands) - 1),
        out_specs=jax.tree.map(lambda _: HBM, out_shape),
        scratch_shapes=scratch,
        cost_estimate=pl.CostEstimate(flops=flops, bytes_accessed=16 * 2**20, transcendentals=0),
        compiler_params=pltpu.CompilerParams(vmem_limit_bytes=VMEM_GRANT),
        name=name,
    )(*operands)


class Copies:
    def __init__(self, semaphores):
        self.semaphores, self.used = semaphores, 0

    def start(self, source, target):
        copy = pltpu.make_async_copy(source, target, self.semaphores.at[self.used])
        self.used += 1
        copy.start()
        return copy

    def start_either(self, first, zero_source, one_source, target):
        semaphore = self.semaphores.at[self.used]
        self.used += 1

        @pl.when(first)
        def _():
            pltpu.make_async_copy(zero_source, target, semaphore).start()

        @pl.when(jnp.logical_not(first))
        def _():
            pltpu.make_async_copy(one_source, target, semaphore).start()

        return pltpu.make_async_copy(zero_source, target, semaphore)


def rows_from(position, distance, row_count, count):
    source = lax.rem(position - distance + count, count)
    return pl.ds(pl.multiple_of(source * row_count, row_count), row_count)


def orthonormalize(power_ref, q_ref, gram_ref):
    bf16 = jnp.bfloat16
    width = gram_ref.shape[0]
    for start in range(0, power_ref.shape[1], width):
        span = slice(start, start + width)
        group = power_ref[:, span]
        if start > 0:
            along = product(q_ref[:, :start], group.astype(bf16), TN).astype(bf16)
            group = group - product(q_ref[:, :start], along, NN)
        group = (group * lax.rsqrt(jnp.sum(group * group, axis=0, keepdims=True))).astype(bf16)
        gram_ref[...] = product(group, group, TN)
        invert_factor(gram_ref)
        inverse = split_cat(gram_ref[...], "hl", 1)
        q_ref[:, span] = product(jnp.concatenate([group, group], axis=1), inverse, NT).astype(bf16)


def share_kernel(symmetric, place_ref, factor_ref, basis_ref, early_ref, share_ref, late_ref):
    row_count, order = factor_ref.shape
    count = order // row_count
    width = order // 4
    bf16 = jnp.bfloat16
    shared = share_ref.shape[1] - width
    early_ref[...] = basis_ref[:, :width].astype(bf16)
    share_ref[:, shared:] = basis_ref[:, width : 2 * width].astype(bf16)
    late_ref[...] = basis_ref[:, 2 * width :].astype(bf16)
    if not symmetric:
        share_ref[:, :shared] = factor_ref[...].astype(bf16)
        return
    half = row_count // 2
    for r in range(count):

        @pl.when(place_ref[1] == r)
        def _():
            for offset in range(count // 2):
                start = (r + offset) % count * row_count
                share_ref[:, offset * row_count : (offset + 1) * row_count] = factor_ref[
                    :, start : start + row_count
                ].astype(bf16)
            start = (r + count // 2) % count * row_count
            if r < count // 2:
                last = factor_ref[:, start : start + half]
            else:
                last = factor_ref[half:, start : start + row_count].T
            share_ref[:, count // 2 * row_count : shared] = last.astype(bf16)


def gather_shares(place, factor_rows, basis_rows, symmetric):
    row_count, order = factor_rows.shape
    shared = order // 2 + row_count // 2 if symmetric else order
    vmem = pl.BlockSpec(memory_space=pltpu.VMEM)
    return pl.pallas_call(
        functools.partial(share_kernel, symmetric),
        out_shape=tuple(
            jax.ShapeDtypeStruct((row_count, columns), jnp.bfloat16)
            for columns in (order // 4, shared + order // 4, order // 2)
        ),
        in_specs=[SMEM, vmem, vmem],
        out_specs=(vmem,) * 3,
        cost_estimate=pl.CostEstimate(flops=0, bytes_accessed=3 * 2**20, transcendentals=0),
        compiler_params=pltpu.CompilerParams(vmem_limit_bytes=VMEM_GRANT),
        name="gather_shares",
    )(place, factor_rows, basis_rows)


def first_kernel(half_steps, count, place_ref, gathered_hbm, rows_hbm, *refs):
    own, other, basis = refs[:count], refs[count : 2 * count], refs[2 * count : 3 * count]
    whole_hbm, new_rows_hbm, q_hbm = refs[3 * count : 3 * count + 3]
    block, old, columns, rows, whole, new_rows, power, q, gram, semaphores = refs[3 * count + 3 :]
    row_count, order = rows.shape
    half_width = order // 2
    width = order // 4
    shared = old.shape[1]
    first = place_ref[0] == 0
    copies = Copies(semaphores)
    waits, late = [], []
    for k in range(count):
        span = rows_from(place_ref[1], k, row_count, count)
        waits.append(copies.start_either(first, own[k], other[k], block.at[span, pl.ds(0, half_width)]))
        waits.append(copies.start_either(first, other[k], own[k], block.at[span, pl.ds(half_width, half_width)]))
    waits.append(copies.start(gathered_hbm.at[:, pl.ds(0, shared)], old))
    waits.append(copies.start(rows_hbm, rows))
    late.append(copies.start(gathered_hbm.at[:, pl.ds(shared, width)], columns.at[:, pl.ds(width, width)]))
    for k in range(count):
        span = rows_from(place_ref[1], k, row_count, count)
        late.append(copies.start(basis[k], columns.at[span, pl.ds(0, width)]))
    for copy in waits:
        copy.wait()

    def old_block(r, c):
        offset = (c - r) % count
        row = slice(r * row_count, (r + 1) * row_count)
        if half_steps is None:
            return old[row, c * row_count : (c + 1) * row_count].astype(jnp.float32)
        if offset < half_steps:
            return old[row, offset * row_count : (offset + 1) * row_count].astype(jnp.float32)
        if offset > half_steps or r >= half_steps:
            return old_block(c, r).T
        mirror = slice(c * row_count, (c + 1) * row_count)
        part = slice(half_steps * row_count, half_steps * row_count + row_count // 2)
        return jnp.concatenate([old[row, part], old[mirror, part]], axis=1).astype(jnp.float32)

    @pl.when(first)
    def _():
        for start in range(0, order, width):
            power[start : start + width, :] = product(block[start : start + width, :], block[...], NT)

    @pl.when(jnp.logical_not(first))
    def _():
        for start in range(0, order, width):
            power[start : start + width, :] = product(block[:, start : start + width], block[...], TN)

    here = rows_from(place_ref[1], 0, row_count, count)
    new_rows[...] = 0.95 * rows[...] + 0.05 * power[here, :]
    for r in range(count):
        row = slice(r * row_count, (r + 1) * row_count)
        rest = jnp.concatenate([old_block(r, c) for c in range(count)], axis=1)
        whole[row, :] = (0.95 * rest + 0.05 * power[row, :]).astype(jnp.bfloat16)
    outputs = [copies.start(new_rows, new_rows_hbm), copies.start(whole, whole_hbm)]
    for copy in late:
        copy.wait()
    power[:, :half_width] = product(whole[...], columns[...], NN)
    orthonormalize(power.at[:, pl.ds(0, half_width)], q, gram)
    outputs.append(copies.start(q, q_hbm))
    for copy in outputs:
        copy.wait()


def first_half(place, own, other, basis, gathered, rows, half_steps):
    row_count, order = rows.shape
    count = len(own)
    half = order // 2
    bf16, f32 = jnp.bfloat16, jnp.float32
    shape, vmem = jax.ShapeDtypeStruct, pltpu.VMEM
    return kernel_call(
        functools.partial(first_kernel, half_steps, count),
        "first_half",
        (shape((order, order), bf16), shape(rows.shape, f32), shape((order, half), bf16)),
        [
            vmem((order, order), bf16),
            vmem((order, gathered.shape[1] - order // 4), bf16),
            vmem((order, half), bf16),
            vmem(rows.shape, f32),
            vmem((order, order), bf16),
            vmem(rows.shape, f32),
            vmem((order, order), f32),
            vmem((order, half), bf16),
            vmem((half // 2, half // 2), f32),
            pltpu.SemaphoreType.DMA((3 * count + 6,)),
        ],
        6 * order**3,
        (place, gathered, rows, *own, *other, *basis),
    )


def second_kernel(row_count, place_ref, columns_hbm, whole_hbm, before_hbm, q_hbm, rows_hbm, *refs):
    whole, before, columns, power, q, gram, semaphores = refs
    order, half = before.shape
    bf16 = jnp.bfloat16
    here = rows_from(place_ref[1], 0, row_count, order // row_count)
    copies = Copies(semaphores)
    waits = [copies.start(whole_hbm, whole), copies.start(columns_hbm, columns)]
    last = copies.start(before_hbm, before)
    for copy in waits:
        copy.wait()
    power[...] = product(whole[...], columns[...], NN)
    last.wait()
    outputs = [copies.start(before.at[here, :], rows_hbm.at[:, pl.ds(0, half)])]
    along = product(before[...], power[...].astype(bf16), TN)
    power[...] = power[...] - product(before[...], along.astype(bf16), NN)
    orthonormalize(power, q, gram)
    outputs.append(copies.start(q, q_hbm))
    outputs.append(copies.start(q.at[here, :], rows_hbm.at[:, pl.ds(half, half)]))
    for copy in outputs:
        copy.wait()


def second_half(place, columns, whole, before, row_count):
    order, half = before.shape
    bf16, f32 = jnp.bfloat16, jnp.float32
    shape, vmem = jax.ShapeDtypeStruct, pltpu.VMEM
    return kernel_call(
        functools.partial(second_kernel, row_count),
        "second_half",
        (shape((order, half), bf16), shape((row_count, order), bf16)),
        [
            vmem((order, order), bf16),
            vmem((order, half), bf16),
            vmem((order, half), bf16),
            vmem((order, half), f32),
            vmem((order, half), bf16),
            vmem((half // 2, half // 2), f32),
            pltpu.SemaphoreType.DMA((6,)),
        ],
        4 * order**3,
        (place, columns, whole, before),
    )


def rotate_kernel(count, place_ref, own_first, own_second, other_first, *refs):
    own_pieces, other_pieces, (mixed_hbm, upper_hbm) = refs[:count], refs[count : 2 * count], refs[2 * count : 2 * count + 2]
    left, right, block, mixed, rotated, semaphores = refs[2 * count + 2 :]
    order, half_width = left.shape
    first = place_ref[0] == 0
    upper, lower = pl.ds(0, half_width), pl.ds(half_width, half_width)
    copies = Copies(semaphores)
    waits = [copies.start_either(first, other_first, own_second, right)]
    for k in range(count):
        span = rows_from(place_ref[1], k, order // count, count)
        waits.append(copies.start_either(first, own_pieces[k], other_pieces[k], block.at[span, upper]))
        waits.append(copies.start_either(first, other_pieces[k], own_pieces[k], block.at[span, lower]))
    last = copies.start_either(first, own_first, other_first, left)
    for copy in waits:
        copy.wait()
    mixed[...] = product(block[...], right[...], NN).astype(mixed.dtype)
    outputs = [copies.start(mixed, mixed_hbm)]
    last.wait()
    rotated[...] = product(left[...], mixed[...], TN)
    outputs.append(copies.start(rotated, upper_hbm))
    for copy in outputs:
        copy.wait()


def rotate_step(place, own, other_first, own_pieces, other_pieces):
    order, half = other_first.shape
    count = len(own_pieces)
    shape, vmem = jax.ShapeDtypeStruct, pltpu.VMEM
    bf16, f32 = jnp.bfloat16, jnp.float32
    columns = vmem((order, half), bf16)
    return kernel_call(
        functools.partial(rotate_kernel, count),
        "rotate_step",
        (shape((order, half), bf16), shape((half, half), f32)),
        [
            columns,
            columns,
            vmem((order, order), bf16),
            columns,
            vmem((half, half), f32),
            pltpu.SemaphoreType.DMA((2 * count + 4,)),
        ],
        2 * order * order * half + 2 * order * half * half,
        (place, *own, other_first, *own_pieces, *other_pieces),
    )


def moment_kernel(place_ref, *refs):
    own, other, (mixed_hbm, upper_hbm, moments_hbm, first_hbm, second_hbm) = refs[:2], refs[2:4], refs[4:9]
    near_hbm, far_hbm, first_out, second_out = refs[9:13]
    left, left_rows, right, moments, first_rows, second_rows, mixed, rotated, normal, near, far, semaphores = refs[13:]
    row_count, half_width = first_rows.shape
    order = left.shape[0]
    f32, bf16 = jnp.float32, jnp.bfloat16
    first = place_ref[0] == 0
    here = rows_from(place_ref[1], 0, row_count, order // row_count)
    upper, lower = pl.ds(0, half_width), pl.ds(half_width, half_width)
    copies = Copies(semaphores)
    waits = [
        copies.start(moments_hbm, moments),
        copies.start(upper_hbm, rotated.at[upper, :]),
        copies.start_either(first, own[0].at[here, :], other[0].at[here, :], left_rows.at[:, upper]),
        copies.start_either(first, own[1].at[here, :], other[1].at[here, :], left_rows.at[:, lower]),
    ]
    late = [
        copies.start(mixed_hbm, mixed),
        copies.start_either(first, own[1], other[1], left),
        copies.start(first_hbm, first_rows),
        copies.start(second_hbm, second_rows),
        copies.start_either(first, other[0], own[1], right),
    ]
    for copy in waits:
        copy.wait()
    total = jnp.zeros(near.shape, f32)
    width = order // 4
    for start in range(0, order, width):
        span = slice(start, start + width)
        if start == half_width:
            for copy in late:
                copy.wait()
        if start >= half_width:
            rotated[span, :] = product(left[:, start - half_width : start - half_width + width], mixed[...], TN)
        turn = rotated[span, :]
        new_first = 0.95 * moments[span, :half_width].astype(f32) + 0.05 * turn
        new_second = 0.95 * moments[span, half_width:].astype(f32) + 0.05 * turn * turn
        normal[span, :] = (new_first / (jnp.sqrt(new_second) + 1e-08)).astype(bf16)
        total = total + product(left_rows[:, span], normal[span, :], NN)
    part = product(total.astype(bf16), right[...], NT)

    @pl.when(first)
    def _():
        near[...] = part[:, :half_width]
        far[...] = part[:, half_width:].astype(bf16)

    @pl.when(jnp.logical_not(first))
    def _():
        near[...] = part[:, half_width:]
        far[...] = part[:, :half_width].astype(bf16)

    outputs = [copies.start(far, far_hbm), copies.start(near, near_hbm)]
    turn = rotated[here, :]
    first_rows[...] = 0.95 * first_rows[...] + 0.05 * turn
    second_rows[...] = 0.95 * second_rows[...] + 0.05 * turn * turn
    outputs += [copies.start(first_rows, first_out), copies.start(second_rows, second_out)]
    for copy in outputs:
        copy.wait()


def moment_step(place, own, other, mixed, upper, moments, first, second):
    order = own[0].shape[0]
    half = first.shape[1]
    f32, bf16 = jnp.float32, jnp.bfloat16
    shape, vmem = jax.ShapeDtypeStruct, pltpu.VMEM
    return kernel_call(
        moment_kernel,
        "moment_step",
        (shape(first.shape, f32), shape(first.shape, bf16), shape(first.shape, f32), shape(first.shape, f32)),
        [
            vmem((order, half), bf16),
            vmem((first.shape[0], order), bf16),
            vmem((order, half), bf16),
            vmem((order, order), bf16),
            vmem(first.shape, f32),
            vmem(first.shape, f32),
            vmem((order, half), bf16),
            vmem((order, half), f32),
            vmem((order, half), bf16),
            vmem(first.shape, f32),
            vmem(first.shape, bf16),
            pltpu.SemaphoreType.DMA((13,)),
        ],
        2 * order * half * half,
        (place, *own, *other, mixed, upper, moments, first, second),
    )


def exchanged(block, axis, partner_of):
    count = lax.axis_size(axis)
    return lax.ppermute(block, axis, [(i, partner_of(i)) for i in range(count)])


def sibling(block):
    return exchanged(block, "dp", lambda i: i ^ 1)


def rounded_sum(x, y):
    return (x.astype(jnp.float32) + y.astype(jnp.float32)).astype(jnp.bfloat16)


def reversed_bits(value, bits):
    return sum(((value >> k) & 1) << (bits - 1 - k) for k in range(bits))


def pair_terms(partial_rows, half_width):
    side = lax.axis_index("dp") % 2
    blocks = lax.axis_size("dp") // 2
    bits = blocks.bit_length() - 1
    row_blocks, _, columns = partial_rows.shape
    halves = [
        partial_rows[rb, :, start : start + half_width]
        for rb in range(row_blocks)
        for start in range(0, columns, half_width)
    ]
    lows, highs = halves[0::2], halves[1::2]
    turned = [reversed_bits(k, bits) for k in range(blocks)]
    keep = jnp.stack([jnp.where(side == 0, lows[k], highs[turned[k]]) for k in range(blocks)])
    send = jnp.stack([jnp.where(side == 0, highs[turned[k]], lows[k]) for k in range(blocks)])
    return send, keep


def reduced_half_block(held, ahead):
    position = lax.axis_index("dp")
    side = position % 2
    bits = held.shape[0].bit_length() - 1
    for step in range(bits):
        low_bit, high_bit = 1 + step, bits - step
        mine = jnp.where(side == 0, position >> high_bit, position >> low_bit) & 1
        middle = held.shape[0] // 2
        keep = jnp.where(mine == 0, held[:middle], held[middle:])
        send = jnp.where(mine == 0, held[middle:], held[:middle])
        if step == 0:
            send, ahead = lax.optimization_barrier((send, ahead))
        arrived = exchanged(send, "dp", lambda i: i ^ (1 << (low_bit if i % 2 else high_bit)))
        held = rounded_sum(keep, arrived)
    return held[0], ahead


def pieces_by_distance(shard, axis):
    count = lax.axis_size(axis)
    return [shard] + [
        lax.ppermute(shard, axis, [(i, (i + distance) % count) for i in range(count)]) for distance in range(1, count)
    ]


def body(grad_partial, factors, bases, first_moment, second_moment):
    row_count, block_width = factors.shape[1:]
    half_width = block_width // 2
    side = lax.axis_index("dp") % 2
    position, count = lax.axis_index("fsdp"), lax.axis_size("fsdp")
    place = jnp.stack([side, position]).astype(jnp.int32)
    bf16 = jnp.bfloat16

    symmetric = row_count % 256 == 0 and count % 2 == 0
    early, share, late = gather_shares(place, factors[0], bases[0], symmetric)
    first_pieces = pieces_by_distance(early, "fsdp")
    gathered = lax.all_gather(share, "fsdp", axis=0, tiled=True)
    late = lax.all_gather(late, "fsdp", axis=0, tiled=True)
    send, keep = pair_terms(grad_partial[0], half_width)
    pair_sum = rounded_sum(keep, sibling(send))
    own_half, first_pieces = reduced_half_block(pair_sum, first_pieces)
    moments = jnp.concatenate([first_moment[0].astype(bf16), second_moment[0].astype(bf16)], axis=1)
    moments, own_half = lax.optimization_barrier((moments, own_half))
    moments = lax.all_gather(moments, "fsdp", axis=0, tiled=True)
    own_pieces = pieces_by_distance(own_half, "fsdp")
    other_pieces = [sibling(piece) for piece in own_pieces]

    factor_whole, new_factor_rows, first_q = first_half(
        place, own_pieces, other_pieces, first_pieces, gathered, factors[0], count // 2 if symmetric else None
    )
    first_other = sibling(first_q)
    second_q, new_rows = second_half(place, late, factor_whole, first_q, row_count)
    own, other = (first_q, second_q), (first_other, sibling(second_q))
    mixed, upper = rotate_step(place, own, first_other, own_pieces, other_pieces)
    near, far, first_new, second_new = moment_step(
        place, own, other, mixed, upper, moments, first_moment[0], second_moment[0]
    )
    direction = (near + sibling(far).astype(jnp.float32)).astype(bf16)
    return (new_factor_rows[None], new_rows[None], first_new[None], second_new[None], direction[None])


def solution(mesh):
    rows = P("dp", "fsdp", None)
    return jax.shard_map(
        body,
        mesh=mesh,
        in_specs=(P("dp", None, "fsdp", None), rows, rows, rows, rows),
        out_specs=(rows,) * 5,
        check_vma=False,
    )
```
